1024 devices in a mesh: fsdp: 128 (over z, y_hi, x), head: 8 (over y_lo, core).
Axes of the slice: x: 4, y: 8 (y_hi: 2, y_lo: 4; y = y_hi * 4 + y_lo), z: 16, core: 2. Of those that a mesh axis runs over, the one named last changes fastest.
Arguments:
- tokens: bfloat16 [32768, 5120], P(('fsdp', 'head')), may hold values from -6 to 6
- positions: int32 [32768], P(('fsdp', 'head')), may hold values from 0 to 2046, as said below
- offsets: int32 [32768], P(('fsdp', 'head')), may hold values from 0 to 32767, as said below
- q_weight: bfloat16 [5120, 2048], P('fsdp', 'head'), may hold values from -0.078125 to 0.078125
- x_weight: bfloat16 [5120, 2048], P('fsdp', 'head'), may hold values from -0.078125 to 0.078125
- shared_weight: bfloat16 [5120, 1024], P('fsdp', 'head'), may hold values from -0.078125 to 0.078125
- conv_x: float32 [4, 2048], P(None, 'head'), may hold values from -3 to 3
- conv_bc: float32 [4, 512], replicated, may hold values from -3 to 3
Outputs:
- q_rot: bfloat16 [32768, 2048], P('fsdp', 'head')
- k_rot: bfloat16 [32768, 512], P('fsdp')
- x_conv: bfloat16 [32768, 2048], P('fsdp', 'head')
- bc_conv: bfloat16 [32768, 512], P('fsdp')
The draws below stay inside these ranges and needn't reach their ends.
Inputs may be any that keep to these rules, and one draw needn't show every extreme that they name: positions rise by one from row to row within a sequence. offsets[t] is the first row of row t's sequence; offsets[t] <= t and t - offsets[t] < 1024; sequences are runs of consecutive rows; the last row begins a sequence of its own.
All inputs are finite; a program needn't handle non-finite values.
Results may differ from the reference program's by a relative error of at most 0.012.
Values may be sent and summed in bfloat16 or wider, within the bound.
No kernel may reach another device: no remote copies, remote signals or barrier semaphores. Data moves between devices by JAX's collectives and lax.ppermute only.
A program may use at most 32 MiB of HBM per device.

```python
import jax
import jax.numpy as jnp
from jax import lax

D = 5120
HD = 128
KH = 4
STATE = 256
TAPS = 4
QH = 16
XC = 2048
SHARED = 1024
TOKENS = 32768


def doc_layout(key):
    row_ids = jnp.arange(TOKENS, dtype=jnp.int32)
    period = min(1024, TOKENS // 2)
    spread = max(8, period // 4)
    marks = jax.random.randint(jax.random.fold_in(key, 11), (TOKENS,), 0, spread)
    starts = (marks == 0) | (row_ids % period == 0) | (row_ids == TOKENS - 1)
    starts = starts & ((row_ids >= period) | (row_ids == 0))
    firsts = lax.cummax(jnp.where(starts, row_ids, 0), axis=0)
    bases = jax.random.randint(jax.random.fold_in(key, 12), (TOKENS,), 0, period)
    bases = jnp.where(row_ids == 0, period - 1, jnp.where(row_ids == period, 0, bases))
    places = row_ids - firsts + bases[firsts]
    return (places.astype(jnp.int32), firsts.astype(jnp.int32))


def draw_positions(key, part):
    layout = doc_layout(key)
    return layout[0]


def draw_offsets(key, part):
    layout = doc_layout(key)
    return layout[1]


def steps_of(rng, extent, cuts, smallest, top_value):
    factor_of = 1.0
    for dim, parts in cuts:
        heights = jax.random.uniform(jax.random.fold_in(jax.random.fold_in(rng, 6), dim), (parts,), jnp.float32, smallest / len(cuts), top_value / len(cuts))
        factor_of = factor_of * jnp.repeat(jnp.exp(heights), extent[dim] // parts).reshape((-1,) + (1,) * (len(extent) - 1 - dim))
    return factor_of


def centred(own_key, extent, scale, reach, cuts=(), held_as=jnp.bfloat16):
    array = scale * jax.random.normal(own_key, extent, jnp.float32)
    if cuts:
        array = array * steps_of(own_key, extent, cuts, -0.22, 0.18)
    return jnp.clip(array, -reach, reach).astype(held_as)


def setup_inputs(seed: int = 0) -> dict:
    streams_of = jax.random.split(jax.random.key(seed), 9)
    return {
        "tokens": centred(streams_of[0], (TOKENS, D), 1.0, 6.0, ((0, 1024),)),
        "positions": draw_positions(jax.random.fold_in(streams_of[8], 71), 0),
        "offsets": draw_offsets(jax.random.fold_in(streams_of[8], 71), 0),
        "q_weight": centred(streams_of[3], (D, QH * HD), D ** -0.5, 0.078125, ((0, 128), (1, 8))),
        "x_weight": centred(streams_of[4], (D, XC), D ** -0.5, 0.078125, ((0, 128), (1, 8))),
        "shared_weight": centred(streams_of[5], (D, SHARED), D ** -0.5, 0.078125, ((0, 128), (1, 8))),
        "conv_x": centred(streams_of[6], (TAPS, XC), 0.5, 3.0, ((1, 8),), jnp.float32),
        "conv_bc": centred(streams_of[7], (TAPS, 2 * STATE), 0.5, 3.0, (), jnp.float32),
    }


rope_base = 10000.0


def rotate(values, places, head_size):
    count_rows = values.shape[0]
    heads = values.reshape(count_rows, -1, head_size)
    half = head_size // 2
    index = jnp.arange(half, dtype=jnp.float32)
    inverse = jnp.exp(-jnp.log(jnp.float32(rope_base)) * index / jnp.float32(half))
    angle = places.astype(jnp.float32)[:, None] * inverse[None, :]
    cosine = jnp.cos(angle)[:, None, :]
    sine = jnp.sin(angle)[:, None, :]
    first = heads[..., :half]
    second = heads[..., half:]
    turned = jnp.concatenate([first * cosine - second * sine, second * cosine + first * sine], axis=-1)
    return turned.reshape(count_rows, -1)


def causal_conv(extended, taps, row_ids, starts):
    lag_rows = taps.shape[0] - 1
    count_rows = row_ids.shape[0]
    total = jnp.zeros((count_rows, extended.shape[1]), jnp.float32)
    for step_back in range(taps.shape[0]):
        window = extended[lag_rows - step_back: lag_rows - step_back + count_rows].astype(jnp.float32)
        valid = (row_ids - step_back >= starts).astype(jnp.float32)
        total = total + taps[step_back][None, :] * window * valid[:, None]
    return jax.nn.silu(total).astype(jnp.bfloat16)


def reference(tokens, positions, offsets, q_weight, x_weight, shared_weight, conv_x, conv_bc):
    q_proj = jnp.dot(tokens, q_weight, preferred_element_type=jnp.float32).astype(jnp.bfloat16)
    x_proj = jnp.dot(tokens, x_weight, preferred_element_type=jnp.float32).astype(jnp.bfloat16)
    s_proj = jnp.dot(tokens, shared_weight, preferred_element_type=jnp.float32).astype(jnp.bfloat16)
    q_rot = rotate(q_proj.astype(jnp.float32), positions, HD).astype(jnp.bfloat16)
    k_rot = rotate(s_proj[:, :KH * HD].astype(jnp.float32), positions, HD).astype(jnp.bfloat16)
    row_ids = jnp.arange(TOKENS, dtype=jnp.int32)
    lag_rows = TAPS - 1
    x_ext = jnp.concatenate([jnp.zeros((lag_rows, XC), jnp.bfloat16), x_proj], axis=0)
    bc_ext = jnp.concatenate([jnp.zeros((lag_rows, 2 * STATE), jnp.bfloat16), s_proj[:, KH * HD:]], axis=0)
    x_conv = causal_conv(x_ext, conv_x, row_ids, offsets)
    bc_conv = causal_conv(bc_ext, conv_bc, row_ids, offsets)
    return (q_rot, k_rot, x_conv, bc_conv)
```

```python
import jax
import jax.numpy as jnp
from jax import lax
from jax.experimental import pallas as pl
from jax.experimental.pallas import tpu as pltpu
from jax.sharding import Mesh, PartitionSpec as P

HD = 128
KH = 4
HALO = 16
rope_base = 10000.0

AXES = ("zh", "zl", "yh", "x", "yl", "c")
SIZES = (4, 4, 2, 4, 4, 2)
FSDP = AXES[:4]


def fsdp_index(zh, zl, yh, x):
    return ((zh * 4 + zl) * 2 + yh) * 4 + x


def weight_moves(flip):
    moves = []
    for zh in range(4):
        for zl in range(4):
            for yh in range(2):
                for x in range(4):
                    inner = 2 * (zh % 2) + (yh if not flip else 1 - yh)
                    moves.append((fsdp_index(x, zl, zh // 2, inner), fsdp_index(zh, zl, yh, x)))
    return moves


def partial_kernel(core_ref, own_ref, other_ref, w_ref, out_ref, w_vmem, sems):
    copies = []
    for zh in range(4):
        for zl in range(4):
            copies.append(
                pltpu.make_async_copy(
                    w_ref.at[pl.ds((zh * 4 + zl) * 80, 80)],
                    w_vmem.at[pl.ds((zl * 4 + zh) * 80, 80)],
                    sems.at[zh * 4 + zl],
                )
            )
    for copy in copies:
        copy.start()
    for copy in copies:
        copy.wait()
    core = core_ref[0]
    for rows_ref, place in ((own_ref, core), (other_ref, 1 - core)):
        for first, width in ((0, 256), (256, 256), (512, 128)):
            part = jnp.dot(
                rows_ref[...], w_vmem[:, first : first + width], preferred_element_type=jnp.float32
            ).astype(jnp.bfloat16)
            for x in range(4):
                for yl in range(4):
                    piece = part[(x * 4 + yl) * 32 : (x * 4 + yl + 1) * 32]
                    at = pl.multiple_of(yl * 64 + place * 32, 32)
                    out_ref[x, pl.ds(at, 32), first : first + width] = piece


def final_kernel(
    halo_ref, proj_ref, s_ref, cos_ref, sin_ref, rel_ref, tx_ref, tbc_ref,
    q_ref, k_ref, x_ref, bc_ref, ext_ref,
):
    rows = proj_ref.shape[0]
    cosine = cos_ref[...]
    sine = sin_ref[...]

    def turned(values):
        return (values * cosine + pltpu.roll(values, HD // 2, 1) * sine).astype(jnp.bfloat16)

    def convolved(taps_ref, first):
        total = ext_ref[pl.ds(HALO, rows), :] * taps_ref[0:1, first : first + HD]
        for step_back in range(1, 4):
            window = ext_ref[pl.ds(HALO - step_back, rows), :] * taps_ref[step_back : step_back + 1, first : first + HD]
            total = total + jnp.where(rel_ref[...] >= step_back, window, 0.0)
        return (total / (1.0 + jnp.exp(-total))).astype(jnp.bfloat16)

    for head in range(2):
        cols = slice(head * HD, (head + 1) * HD)
        q_ref[:, cols] = turned(proj_ref[:, cols].astype(jnp.float32))
    for head in range(KH):
        k_ref[:, head * HD : (head + 1) * HD] = turned(s_ref[head, HALO:, :].astype(jnp.float32))
    for block in range(2):
        cols = slice(256 + block * HD, 256 + (block + 1) * HD)
        ext_ref[0:HALO, :] = halo_ref[:, cols].astype(jnp.float32)
        ext_ref[HALO:, :] = proj_ref[:, cols].astype(jnp.float32)
        x_ref[:, block * HD : (block + 1) * HD] = convolved(tx_ref, block * HD)
    for block in range(4):
        ext_ref[...] = s_ref[KH + block].astype(jnp.float32)
        bc_ref[:, block * HD : (block + 1) * HD] = convolved(tbc_ref, block * HD)


def shards(tokens, positions, offsets, q_weight, x_weight, shared_weight, conv_x, conv_bc):
    bf16 = jnp.bfloat16
    weight = jnp.concatenate([q_weight, x_weight, shared_weight], axis=1)
    own_w = lax.ppermute(weight, FSDP, weight_moves(False))
    other_w = lax.ppermute(weight, FSDP, weight_moves(True))
    low = lax.axis_index("yh") == 0
    pair = jnp.concatenate([jnp.where(low, own_w, other_w), jnp.where(low, other_w, own_w)], axis=0)
    quarter = lax.all_gather(pair, ("zh", "zl"), axis=0, tiled=True)

    rows, width = tokens.shape
    split = tokens.reshape(rows, 4, width // 4).transpose(1, 0, 2)
    split = jnp.broadcast_to(split[:, None], (4, 4, rows, width // 4)).reshape(16, rows, width // 4)
    own_t = lax.all_to_all(split, ("x", "yl"), 0, 0).reshape(16 * rows, width // 4)
    other_t = lax.ppermute(own_t, "c", [(0, 1), (1, 0)])

    places = lax.all_gather(jnp.stack([positions, offsets]), ("yl", "c"), axis=1, tiled=True)
    group_rows = places.shape[1]
    half = HD // 2
    index = jnp.arange(half, dtype=jnp.float32)
    inverse = jnp.exp(-jnp.log(jnp.float32(rope_base)) * index / jnp.float32(half))
    angle = places[0].astype(jnp.float32)[:, None] * inverse[None, :]
    cosine, sine = jnp.cos(angle), jnp.sin(angle)
    cosine = jnp.concatenate([cosine, cosine], axis=1)
    sine = jnp.concatenate([-sine, sine], axis=1)
    row_ids = lax.axis_index(FSDP) * group_rows + jnp.arange(group_rows, dtype=jnp.int32)
    rel = jnp.broadcast_to((row_ids - places[1])[:, None], (group_rows, HD))

    columns = weight.shape[1]
    core = lax.axis_index("c").astype(jnp.int32).reshape(1)
    vmem = pl.BlockSpec(memory_space=pltpu.VMEM)
    partial = pl.pallas_call(
        partial_kernel,
        out_shape=jax.ShapeDtypeStruct((4, group_rows, columns), bf16),
        in_specs=[
            pl.BlockSpec(memory_space=pltpu.SMEM), vmem, vmem, pl.BlockSpec(memory_space=pl.ANY),
        ],
        out_specs=vmem,
        scratch_shapes=[pltpu.VMEM((width // 4, columns), bf16), pltpu.SemaphoreType.DMA((16,))],
        compiler_params=pltpu.CompilerParams(vmem_limit_bytes=40 * 2**20),
        name="partial_products",
    )(core, own_t, other_t, quarter)
    parts = lax.all_to_all(partial, "x", 0, 0)
    proj = jnp.sum(parts.astype(jnp.float32), axis=0).astype(bf16)

    count = 128
    halo = lax.ppermute(proj[group_rows - HALO :], FSDP, [(i, i + 1) for i in range(count - 1)])
    s_own = jnp.concatenate([halo[:, 512:], proj[:, 512:]], axis=0)
    s_all = lax.all_gather(s_own, ("yl", "c"), axis=0)

    return pl.pallas_call(
        final_kernel,
        out_shape=(
            jax.ShapeDtypeStruct((group_rows, 256), bf16),
            jax.ShapeDtypeStruct((group_rows, 512), bf16),
            jax.ShapeDtypeStruct((group_rows, 256), bf16),
            jax.ShapeDtypeStruct((group_rows, 512), bf16),
        ),
        in_specs=[vmem] * 8,
        out_specs=(vmem,) * 4,
        scratch_shapes=[pltpu.VMEM((group_rows + HALO, HD), jnp.float32)],
        compiler_params=pltpu.CompilerParams(vmem_limit_bytes=40 * 2**20),
        name="rotate_and_convolve",
    )(halo, proj, s_all, cosine, sine, rel, conv_x, conv_bc)


def solution(mesh):
    chips = Mesh(mesh.devices.reshape(SIZES), AXES)
    head = ("yl", "c")
    in_specs = (
        P(AXES, None), P(AXES), P(AXES),
        P(FSDP, head), P(FSDP, head), P(FSDP, head),
        P(None, head), P(),
    )
    out_specs = (P(FSDP, head), P(FSDP, None), P(FSDP, head), P(FSDP, None))
    return jax.shard_map(shards, mesh=chips, in_specs=in_specs, out_specs=out_specs, check_vma=False)
```

```python
import jax
import jax.numpy as jnp
from jax import lax
from jax.experimental import pallas as pl
from jax.experimental.pallas import tpu as pltpu
from jax.sharding import Mesh, PartitionSpec as P

HD = 128
KH = 4
HALO = 16
rope_base = 10000.0

AXES = ("zh", "zl", "yh", "x", "yl", "c")
SIZES = (4, 4, 2, 4, 4, 2)
FSDP = AXES[:4]


def fsdp_index(zh, zl, yh, x):
    return ((zh * 4 + zl) * 2 + yh) * 4 + x


def weight_moves(flip):
    moves = []
    for zh in range(4):
        for zl in range(4):
            for yh in range(2):
                for x in range(4):
                    inner = 2 * (zh % 2) + (yh if not flip else 1 - yh)
                    moves.append((fsdp_index(x, zl, zh // 2, inner), fsdp_index(zh, zl, yh, x)))
    return moves


def shifted(count, steps):
    return [((i + steps) % count, i) for i in range(count)]


def partial_kernel(
    place_ref, own_ref, other_ref, tail_ref, w0_ref, up_ref, down_ref, up2_ref, down2_ref, out_ref, w_vmem, sems
):
    core, zl = place_ref[0], place_ref[1]
    copies = []
    for source, step, offset in (
        (w0_ref, 0, 0), (up_ref, 1, 0), (down_ref, 3, 0), (up2_ref, 2, 0), (down2_ref, 2, 160),
    ):
        first = pl.multiple_of(lax.rem(zl + step, 4) * 320 + offset, 32)
        copies.append(
            pltpu.make_async_copy(source, w_vmem.at[pl.ds(first, source.shape[0])], sems.at[len(copies)])
        )
    for copy in copies:
        copy.start()
    for copy in copies:
        copy.wait()
    for first, width in ((0, 256), (256, 256), (512, 128)):
        cols = slice(first, first + width)
        w = w_vmem[:, cols]
        for mine in (True, False):
            rows = own_ref[...] if mine else jnp.concatenate([other_ref[...], tail_ref[...]], axis=0)
            part = jnp.dot(rows, w, preferred_element_type=jnp.float32).astype(jnp.bfloat16)
            place = core if mine else 1 - core
            for x in range(4):
                for yl in range(4):
                    at = pl.multiple_of(HALO + yl * 64 + place * 32, 16)
                    out_ref[x, pl.ds(at, 32), cols] = part[(x * 4 + yl) * 32 : (x * 4 + yl + 1) * 32]
            if not mine:
                out_ref[0, 0:HALO, cols] = part[512 : 512 + HALO]
    for x in range(3):
        out_ref[x + 1, 0:HALO, :] = out_ref[x, 256 : 256 + HALO, :]


def final_kernel(
    core_ref, proj_ref, own_ref, other_ref, cos_ref, sin_ref, rel_ref, tx_ref, tbc_ref,
    q_ref, k_ref, x_ref, bc_ref, ext_ref,
):
    rows = q_ref.shape[0]
    core = core_ref[0]
    cosine = cos_ref[...]
    sine = sin_ref[...]

    def turned(values):
        return (values * cosine + pltpu.roll(values, HD // 2, 1) * sine).astype(jnp.bfloat16)

    def convolved(taps_ref, cols):
        taps = taps_ref[:, cols]
        total = ext_ref[pl.ds(HALO, rows), :] * taps[0:1]
        for step_back in range(1, 4):
            window = ext_ref[pl.ds(HALO - step_back, rows), :] * taps[step_back : step_back + 1]
            total = total + jnp.where(rel_ref[...] >= step_back, window, 0.0)
        return (total / (1.0 + jnp.exp(-total))).astype(jnp.bfloat16)

    for block in range(2):
        cols = slice(block * HD, (block + 1) * HD)
        q_ref[:, cols] = turned(proj_ref[HALO:, cols].astype(jnp.float32))
    for block in range(2):
        cols = slice(block * HD, (block + 1) * HD)
        ext_ref[...] = proj_ref[:, 256 + block * HD : 256 + (block + 1) * HD].astype(jnp.float32)
        x_ref[:, cols] = convolved(tx_ref, cols)
    for s_ref, place in ((own_ref, core), (other_ref, 1 - core)):
        for yl in range(2):
            cols = pl.ds(pl.multiple_of((2 * yl + place) * HD, HD), HD)
            k_ref[:, cols] = turned(s_ref[yl, HALO:, :].astype(jnp.float32))
            ext_ref[...] = s_ref[2 + yl].astype(jnp.float32)
            bc_ref[:, cols] = convolved(tbc_ref, cols)


def shards(tokens, positions, offsets, q_weight, x_weight, shared_weight, conv_x, conv_bc):
    bf16 = jnp.bfloat16
    rows, width = tokens.shape
    quarter = width // 4
    weight = jnp.concatenate([q_weight, x_weight, shared_weight], axis=1)
    depth, columns = weight.shape
    own_w = lax.ppermute(weight, FSDP, weight_moves(False))
    other_w = lax.ppermute(weight, FSDP, weight_moves(True))
    low = lax.axis_index("yh") == 0
    pair = jnp.concatenate([jnp.where(low, own_w, other_w), jnp.where(low, other_w, own_w)], axis=0)

    tokens, pair = lax.optimization_barrier((tokens, pair))
    split = tokens.reshape(rows, 4, quarter).transpose(1, 0, 2)
    split = jnp.broadcast_to(split[:, None], (4, 4, rows, quarter)).reshape(16, rows, quarter)
    own_t = lax.all_to_all(split, ("x", "yl"), 0, 0).reshape(16 * rows, quarter)

    far = [pair] + [lax.ppermute(pair, "zh", shifted(4, steps)) for steps in (1, 2, 3)]
    turn = lax.rem(4 - lax.axis_index("zh"), 4) * (2 * depth)
    near = lax.dynamic_slice(jnp.concatenate(far + far[:3], axis=0), (turn, 0), (8 * depth, columns))

    own_t, _ = lax.optimization_barrier((own_t, near))
    other_t = lax.ppermute(own_t, "c", [(0, 1), (1, 0)])

    z = ("zh", "zl")
    up = lax.ppermute(near, z, shifted(16, 1))
    down = lax.ppermute(near, z, shifted(16, -1))
    up2 = lax.ppermute(near[:160], z, shifted(16, 2))
    down2 = lax.ppermute(near[160:], z, shifted(16, -2))

    core = lax.axis_index("c").astype(jnp.int32)
    tail = jnp.where(core == 1, own_t[16 * rows - HALO :], other_t[16 * rows - HALO :])
    tail = lax.ppermute(tail, ("zh", "zl", "yh"), [(i, i + 1) for i in range(31)])

    places = lax.all_gather(jnp.stack([positions, offsets]), ("yl", "c"), axis=1, tiled=True)
    group_rows = places.shape[1]
    half = HD // 2
    index = jnp.arange(half, dtype=jnp.float32)
    inverse = jnp.exp(-jnp.log(jnp.float32(rope_base)) * index / jnp.float32(half))
    angle = places[0].astype(jnp.float32)[:, None] * inverse[None, :]
    cosine, sine = jnp.cos(angle), jnp.sin(angle)
    cosine = jnp.concatenate([cosine, cosine], axis=1)
    sine = jnp.concatenate([-sine, sine], axis=1)
    row_ids = lax.axis_index(FSDP) * group_rows + jnp.arange(group_rows, dtype=jnp.int32)
    rel = jnp.broadcast_to((row_ids - places[1])[:, None], (group_rows, HD))

    vmem = pl.BlockSpec(memory_space=pltpu.VMEM)
    smem = pl.BlockSpec(memory_space=pltpu.SMEM)
    partial = pl.pallas_call(
        partial_kernel,
        out_shape=jax.ShapeDtypeStruct((4, HALO + group_rows, columns), bf16),
        in_specs=[smem, vmem, vmem, vmem] + [pl.BlockSpec(memory_space=pl.ANY)] * 5,
        out_specs=vmem,
        scratch_shapes=[pltpu.VMEM((quarter, columns), bf16), pltpu.SemaphoreType.DMA((5,))],
        compiler_params=pltpu.CompilerParams(vmem_limit_bytes=40 * 2**20),
        name="partial_products",
    )(
        jnp.stack([core, lax.axis_index("zl").astype(jnp.int32)]),
        own_t, other_t, tail, near, up, down, up2, down2,
    )
    parts = lax.all_to_all(partial, "x", 0, 0)
    proj = jnp.sum(parts.astype(jnp.float32), axis=0).astype(bf16)

    s_proj = jnp.broadcast_to(proj[:, 512:], (4, HALO + group_rows, HD))
    own_s = lax.all_to_all(s_proj, "yl", 0, 0)
    other_s = lax.ppermute(own_s, "c", [(0, 1), (1, 0)])

    return pl.pallas_call(
        final_kernel,
        out_shape=(
            jax.ShapeDtypeStruct((group_rows, 256), bf16),
            jax.ShapeDtypeStruct((group_rows, 512), bf16),
            jax.ShapeDtypeStruct((group_rows, 256), bf16),
            jax.ShapeDtypeStruct((group_rows, 512), bf16),
        ),
        in_specs=[smem] + [vmem] * 8,
        out_specs=(vmem,) * 4,
        scratch_shapes=[pltpu.VMEM((group_rows + HALO, HD), jnp.float32)],
        compiler_params=pltpu.CompilerParams(vmem_limit_bytes=40 * 2**20),
        name="rotate_and_convolve",
    )(core.reshape(1), proj, own_s, other_s, cosine, sine, rel, conv_x, conv_bc)


def solution(mesh):
    chips = Mesh(mesh.devices.reshape(SIZES), AXES)
    head = ("yl", "c")
    in_specs = (
        P(AXES, None), P(AXES), P(AXES),
        P(FSDP, head), P(FSDP, head), P(FSDP, head),
        P(None, head), P(),
    )
    out_specs = (P(FSDP, head), P(FSDP, None), P(FSDP, head), P(FSDP, None))
    return jax.shard_map(shards, mesh=chips, in_specs=in_specs, out_specs=out_specs, check_vma=False)
```

```python
import jax
import jax.numpy as jnp
from jax import lax
from jax.experimental import pallas as pl
from jax.experimental.pallas import tpu as pltpu
from jax.sharding import Mesh, PartitionSpec as P

HD = 128
KH = 4
HALO = 16
rope_base = 10000.0

AXES = ("zh", "zl", "yh", "x", "yl", "c")
SIZES = (4, 4, 2, 4, 4, 2)
FSDP = AXES[:4]


def shifted(count, steps):
    return [((i + steps) % count, i) for i in range(count)]


def permute_kernel(tokens_ref, out_ref, stack_ref):
    for p in range(8):
        stack_ref[p * 32 : (p + 1) * 32, :] = tokens_ref[:, p * 640 : (p + 1) * 640]
    source = lax.broadcasted_iota(jnp.int32, (640, 640), 0)
    target = lax.broadcasted_iota(jnp.int32, (640, 640), 1)
    wanted = (target // 40) % 4 * 160 + target // 160 * 40 + target % 40
    pick = jnp.where(source == wanted, 1.0, 0.0).astype(jnp.bfloat16)
    moved = jnp.dot(stack_ref[...], pick, preferred_element_type=jnp.float32)
    for x in range(4):
        piece = jnp.concatenate(
            [moved[p * 32 : (p + 1) * 32, x * 160 : (x + 1) * 160] for p in range(8)], axis=1
        ).astype(jnp.bfloat16)
        for yl in range(4):
            out_ref[x * 4 + yl] = piece


def partial_kernel(
    place_ref, own_ref, other_ref, tail_ref, w0_ref, up_ref, down_ref, up2_ref, down2_ref, out_ref, w_vmem, sems
):
    core, zl = place_ref[0], place_ref[1]
    copies = []
    for source, step, zhs in (
        (w0_ref, 0, range(4)), (up_ref, 1, range(4)), (down_ref, 3, range(4)),
        (up2_ref, 2, range(2)), (down2_ref, 2, range(2, 4)),
    ):
        for at, zh in enumerate(zhs):
            first = pl.multiple_of((zh * 4 + lax.rem(zl + step, 4)) * 80, 16)
            copies.append(
                pltpu.make_async_copy(source.at[pl.ds(at * 80, 80)], w_vmem.at[pl.ds(first, 80)], sems.at[len(copies)])
            )
    for copy in copies:
        copy.start()
    for copy in copies:
        copy.wait()
    for first, width in ((0, 256), (256, 256), (512, 128)):
        cols = slice(first, first + width)
        w = w_vmem[:, cols]
        for mine in (True, False):
            rows = own_ref[...] if mine else jnp.concatenate([other_ref[...], tail_ref[...]], axis=0)
            part = jnp.dot(rows, w, preferred_element_type=jnp.float32).astype(jnp.bfloat16)
            place = core if mine else 1 - core
            for x in range(4):
                for yl in range(4):
                    at = pl.multiple_of(HALO + yl * 64 + place * 32, 16)
                    out_ref[x, pl.ds(at, 32), cols] = part[(x * 4 + yl) * 32 : (x * 4 + yl + 1) * 32]
            if not mine:
                out_ref[0, 0:HALO, cols] = part[512 : 512 + HALO]
    for x in range(3):
        out_ref[x + 1, 0:HALO, :] = out_ref[x, 256 : 256 + HALO, :]


def final_kernel(
    core_ref, proj_ref, own_ref, other_ref, cos_ref, sin_ref, rel_ref, tx_ref, tbc_ref,
    q_ref, k_ref, x_ref, bc_ref, ext_ref,
):
    rows = q_ref.shape[0]
    core = core_ref[0]
    cosine = cos_ref[...]
    sine = sin_ref[...]

    def turned(values):
        return (values * cosine + pltpu.roll(values, HD // 2, 1) * sine).astype(jnp.bfloat16)

    def convolved(taps_ref, cols):
        taps = taps_ref[:, cols]
        total = ext_ref[pl.ds(HALO, rows), :] * taps[0:1]
        for step_back in range(1, 4):
            window = ext_ref[pl.ds(HALO - step_back, rows), :] * taps[step_back : step_back + 1]
            total = total + jnp.where(rel_ref[...] >= step_back, window, 0.0)
        return (total / (1.0 + jnp.exp(-total))).astype(jnp.bfloat16)

    for block in range(2):
        cols = slice(block * HD, (block + 1) * HD)
        q_ref[:, cols] = turned(proj_ref[HALO:, cols].astype(jnp.float32))
    for block in range(2):
        cols = slice(block * HD, (block + 1) * HD)
        ext_ref[...] = proj_ref[:, 256 + block * HD : 256 + (block + 1) * HD].astype(jnp.float32)
        x_ref[:, cols] = convolved(tx_ref, cols)
    for s_ref, place in ((own_ref, core), (other_ref, 1 - core)):
        for yl in range(2):
            cols = pl.ds(pl.multiple_of((2 * yl + place) * HD, HD), HD)
            k_ref[:, cols] = turned(s_ref[yl, HALO:, :].astype(jnp.float32))
            ext_ref[...] = s_ref[2 + yl].astype(jnp.float32)
            bc_ref[:, cols] = convolved(tbc_ref, cols)


def shards(tokens, positions, offsets, q_weight, x_weight, shared_weight, conv_x, conv_bc):
    bf16 = jnp.bfloat16
    rows, width = tokens.shape
    quarter = width // 4
    vmem = pl.BlockSpec(memory_space=pltpu.VMEM)
    smem = pl.BlockSpec(memory_space=pltpu.SMEM)
    weight = jnp.concatenate([q_weight, x_weight, shared_weight], axis=1)
    columns = weight.shape[1]
    near = lax.all_gather(weight, ("zh", "yh"), axis=0, tiled=True)

    z = ("zh", "zl")
    up = lax.ppermute(near, z, shifted(16, 1))
    down = lax.ppermute(near, z, shifted(16, -1))
    up2 = lax.ppermute(near[:160], z, shifted(16, 2))
    down2 = lax.ppermute(near[160:], z, shifted(16, -2))

    tokens, _ = lax.optimization_barrier((tokens, near))
    split = pl.pallas_call(
        permute_kernel,
        out_shape=jax.ShapeDtypeStruct((16, rows, quarter), bf16),
        in_specs=[vmem],
        out_specs=vmem,
        scratch_shapes=[pltpu.VMEM((8 * rows, width // 8), bf16)],
        compiler_params=pltpu.CompilerParams(vmem_limit_bytes=40 * 2**20),
        name="permute_columns",
    )(tokens)
    own_t = lax.all_to_all(split, ("x", "yl"), 0, 0).reshape(16 * rows, quarter)
    own_t, *_ = lax.optimization_barrier((own_t, up, down, up2, down2))
    other_t = lax.ppermute(own_t, "c", [(0, 1), (1, 0)])

    core = lax.axis_index("c").astype(jnp.int32)
    tail = jnp.where(core == 1, own_t[16 * rows - HALO :], other_t[16 * rows - HALO :])
    tail = lax.ppermute(tail, ("zh", "zl", "yh"), [(i, i + 1) for i in range(31)])

    places = lax.all_gather(jnp.stack([positions, offsets]), ("yl", "c"), axis=1, tiled=True)
    group_rows = places.shape[1]
    half = HD // 2
    index = jnp.arange(half, dtype=jnp.float32)
    inverse = jnp.exp(-jnp.log(jnp.float32(rope_base)) * index / jnp.float32(half))
    angle = places[0].astype(jnp.float32)[:, None] * inverse[None, :]
    cosine, sine = jnp.cos(angle), jnp.sin(angle)
    cosine = jnp.concatenate([cosine, cosine], axis=1)
    sine = jnp.concatenate([-sine, sine], axis=1)
    row_ids = lax.axis_index(FSDP) * group_rows + jnp.arange(group_rows, dtype=jnp.int32)
    rel = jnp.broadcast_to((row_ids - places[1])[:, None], (group_rows, HD))

    partial = pl.pallas_call(
        partial_kernel,
        out_shape=jax.ShapeDtypeStruct((4, HALO + group_rows, columns), bf16),
        in_specs=[smem, vmem, vmem, vmem] + [pl.BlockSpec(memory_space=pl.ANY)] * 5,
        out_specs=vmem,
        scratch_shapes=[pltpu.VMEM((quarter, columns), bf16), pltpu.SemaphoreType.DMA((16,))],
        compiler_params=pltpu.CompilerParams(vmem_limit_bytes=40 * 2**20),
        name="partial_products",
    )(
        jnp.stack([core, lax.axis_index("zl").astype(jnp.int32)]),
        own_t, other_t, tail, near, up, down, up2, down2,
    )
    parts = lax.all_to_all(partial, "x", 0, 0)
    proj = jnp.sum(parts.astype(jnp.float32), axis=0).astype(bf16)

    s_proj = jnp.broadcast_to(proj[:, 512:], (4, HALO + group_rows, HD))
    own_s = lax.all_to_all(s_proj, "yl", 0, 0)
    other_s = lax.ppermute(own_s, "c", [(0, 1), (1, 0)])

    return pl.pallas_call(
        final_kernel,
        out_shape=(
            jax.ShapeDtypeStruct((group_rows, 256), bf16),
            jax.ShapeDtypeStruct((group_rows, 512), bf16),
            jax.ShapeDtypeStruct((group_rows, 256), bf16),
            jax.ShapeDtypeStruct((group_rows, 512), bf16),
        ),
        in_specs=[smem] + [vmem] * 8,
        out_specs=(vmem,) * 4,
        scratch_shapes=[pltpu.VMEM((group_rows + HALO, HD), jnp.float32)],
        compiler_params=pltpu.CompilerParams(vmem_limit_bytes=40 * 2**20),
        name="rotate_and_convolve",
    )(core.reshape(1), proj, own_s, other_s, cosine, sine, rel, conv_x, conv_bc)


def solution(mesh):
    chips = Mesh(mesh.devices.reshape(SIZES), AXES)
    head = ("yl", "c")
    in_specs = (
        P(AXES, None), P(AXES), P(AXES),
        P(FSDP, head), P(FSDP, head), P(FSDP, head),
        P(None, head), P(),
    )
    out_specs = (P(FSDP, head), P(FSDP, None), P(FSDP, head), P(FSDP, None))
    return jax.shard_map(shards, mesh=chips, in_specs=in_specs, out_specs=out_specs, check_vma=False)
```

```python
import jax
import jax.numpy as jnp
from jax import lax
from jax.experimental import pallas as pl
from jax.experimental.pallas import tpu as pltpu
from jax.sharding import Mesh, PartitionSpec as P

HD = 128
KH = 4
HALO = 16
rope_base = 10000.0

AXES = ("zh", "zl", "yh", "x", "yl", "c")
SIZES = (4, 4, 2, 4, 4, 2)
FSDP = AXES[:4]


def permute_kernel(tokens_ref, out_ref, stack_ref):
    for p in range(8):
        stack_ref[p * 32 : (p + 1) * 32, :] = tokens_ref[:, p * 640 : (p + 1) * 640]
    source = lax.broadcasted_iota(jnp.int32, (640, 640), 0)
    target = lax.broadcasted_iota(jnp.int32, (640, 640), 1)
    wanted = target // 40 % 2 * 320 + target // 80 % 2 * 160 + target // 160 * 40 + target % 40
    pick = jnp.where(source == wanted, 1.0, 0.0).astype(jnp.bfloat16)
    moved = jnp.dot(stack_ref[...], pick, preferred_element_type=jnp.float32)
    for x in range(4):
        piece = jnp.concatenate(
            [
                moved[p * 32 : (p + 1) * 32, x * 160 + yh * 80 : x * 160 + (yh + 1) * 80]
                for yh in range(2)
                for p in range(8)
            ],
            axis=1,
        ).astype(jnp.bfloat16)
        for yl in range(4):
            out_ref[x * 4 + yl] = piece


def partial_kernel(place_ref, own_ref, other_ref, tail_ref, w_own_ref, w_other_ref, out_ref):
    core, yh = place_ref[0], place_ref[1]
    half = w_own_ref.shape[0]
    near = pl.ds(pl.multiple_of(yh * half, 128), half)
    far = pl.ds(pl.multiple_of((1 - yh) * half, 128), half)
    for first, width in ((0, 256), (256, 256), (512, 128)):
        cols = slice(first, first + width)
        for mine in (True, False):
            part = 0.0
            for at_k, w_ref in ((near, w_own_ref), (far, w_other_ref)):
                rows = own_ref[:, at_k]
                if not mine:
                    rows = jnp.concatenate([other_ref[:, at_k], tail_ref[:, at_k]], axis=0)
                part = part + jnp.dot(rows, w_ref[:, cols], preferred_element_type=jnp.float32)
            part = part.astype(jnp.bfloat16)
            place = core if mine else 1 - core
            for x in range(4):
                for yl in range(4):
                    at = pl.multiple_of(HALO + yl * 64 + place * 32, 16)
                    out_ref[x, pl.ds(at, 32), cols] = part[(x * 4 + yl) * 32 : (x * 4 + yl + 1) * 32]
            if not mine:
                out_ref[0, 0:HALO, cols] = part[512 : 512 + HALO]
    for x in range(3):
        out_ref[x + 1, 0:HALO, :] = out_ref[x, 256 : 256 + HALO, :]


def final_kernel(
    core_ref, proj_ref, own_ref, other_ref, cos_ref, sin_ref, rel_ref, tx_ref, tbc_ref,
    q_ref, k_ref, x_ref, bc_ref, ext_ref,
):
    rows = q_ref.shape[0]
    core = core_ref[0]
    cosine = cos_ref[...]
    sine = sin_ref[...]

    def turned(values):
        return (values * cosine + pltpu.roll(values, HD // 2, 1) * sine).astype(jnp.bfloat16)

    def convolved(taps_ref, cols):
        taps = taps_ref[:, cols]
        total = ext_ref[pl.ds(HALO, rows), :] * taps[0:1]
        for step_back in range(1, 4):
            window = ext_ref[pl.ds(HALO - step_back, rows), :] * taps[step_back : step_back + 1]
            total = total + jnp.where(rel_ref[...] >= step_back, window, 0.0)
        return (total / (1.0 + jnp.exp(-total))).astype(jnp.bfloat16)

    for block in range(2):
        cols = slice(block * HD, (block + 1) * HD)
        q_ref[:, cols] = turned(proj_ref[HALO:, cols].astype(jnp.float32))
    for block in range(2):
        cols = slice(block * HD, (block + 1) * HD)
        ext_ref[...] = proj_ref[:, 256 + block * HD : 256 + (block + 1) * HD].astype(jnp.float32)
        x_ref[:, cols] = convolved(tx_ref, cols)
    for s_ref, place in ((own_ref, core), (other_ref, 1 - core)):
        for yl in range(2):
            cols = pl.ds(pl.multiple_of((2 * yl + place) * HD, HD), HD)
            k_ref[:, cols] = turned(s_ref[yl, HALO:, :].astype(jnp.float32))
            ext_ref[...] = s_ref[2 + yl].astype(jnp.float32)
            bc_ref[:, cols] = convolved(tbc_ref, cols)


def shards(tokens, positions, offsets, q_weight, x_weight, shared_weight, conv_x, conv_bc):
    bf16 = jnp.bfloat16
    rows, width = tokens.shape
    quarter = width // 4
    vmem = pl.BlockSpec(memory_space=pltpu.VMEM)
    smem = pl.BlockSpec(memory_space=pltpu.SMEM)
    split = pl.pallas_call(
        permute_kernel,
        out_shape=jax.ShapeDtypeStruct((16, rows, quarter), bf16),
        in_specs=[vmem],
        out_specs=vmem,
        scratch_shapes=[pltpu.VMEM((8 * rows, width // 8), bf16)],
        compiler_params=pltpu.CompilerParams(vmem_limit_bytes=40 * 2**20),
        name="permute_columns",
    )(tokens)
    own_t = lax.all_to_all(split, ("x", "yl"), 0, 0).reshape(16 * rows, quarter)

    z = ("zh", "zl")
    weight = jnp.concatenate([q_weight, x_weight, shared_weight], axis=1)
    columns = weight.shape[1]
    partner = lax.ppermute(weight, "yh", [(0, 1), (1, 0)])
    w_own = lax.all_gather(weight, z, axis=0, tiled=True)
    own_t, w_own, partner = lax.optimization_barrier((own_t, w_own, partner))

    other_t = lax.ppermute(own_t, "c", [(0, 1), (1, 0)])
    tail = own_t[16 * rows - HALO :]
    sources = [(2 * i + 1, 2 * i + 2) for i in range(31)]
    tail = lax.ppermute(tail, ("zh", "zl", "yh", "c"), sources) + lax.ppermute(
        tail, ("zh", "zl", "yh", "c"), [(source, target + 1) for source, target in sources]
    )
    w_other = lax.all_gather(partner, z, axis=0, tiled=True)

    core = lax.axis_index("c").astype(jnp.int32)
    places = lax.all_gather(jnp.stack([positions, offsets]), ("yl", "c"), axis=1, tiled=True)
    group_rows = places.shape[1]
    half = HD // 2
    index = jnp.arange(half, dtype=jnp.float32)
    inverse = jnp.exp(-jnp.log(jnp.float32(rope_base)) * index / jnp.float32(half))
    angle = places[0].astype(jnp.float32)[:, None] * inverse[None, :]
    cosine, sine = jnp.cos(angle), jnp.sin(angle)
    cosine = jnp.concatenate([cosine, cosine], axis=1)
    sine = jnp.concatenate([-sine, sine], axis=1)
    row_ids = lax.axis_index(FSDP) * group_rows + jnp.arange(group_rows, dtype=jnp.int32)
    rel = jnp.broadcast_to((row_ids - places[1])[:, None], (group_rows, HD))

    partial = pl.pallas_call(
        partial_kernel,
        out_shape=jax.ShapeDtypeStruct((4, HALO + group_rows, columns), bf16),
        in_specs=[smem] + [vmem] * 5,
        out_specs=vmem,
        compiler_params=pltpu.CompilerParams(vmem_limit_bytes=40 * 2**20),
        name="partial_products",
    )(
        jnp.stack([core, lax.axis_index("yh").astype(jnp.int32)]), own_t, other_t, tail, w_own, w_other,
    )
    parts = lax.all_to_all(partial, "x", 0, 0)
    proj = jnp.sum(parts.astype(jnp.float32), axis=0).astype(bf16)

    s_proj = jnp.broadcast_to(proj[:, 512:], (4, HALO + group_rows, HD))
    own_s = lax.all_to_all(s_proj, "yl", 0, 0)
    other_s = lax.ppermute(own_s, "c", [(0, 1), (1, 0)])

    return pl.pallas_call(
        final_kernel,
        out_shape=(
            jax.ShapeDtypeStruct((group_rows, 256), bf16),
            jax.ShapeDtypeStruct((group_rows, 512), bf16),
            jax.ShapeDtypeStruct((group_rows, 256), bf16),
            jax.ShapeDtypeStruct((group_rows, 512), bf16),
        ),
        in_specs=[smem] + [vmem] * 8,
        out_specs=(vmem,) * 4,
        scratch_shapes=[pltpu.VMEM((group_rows + HALO, HD), jnp.float32)],
        compiler_params=pltpu.CompilerParams(vmem_limit_bytes=40 * 2**20),
        name="rotate_and_convolve",
    )(core.reshape(1), proj, own_s, other_s, cosine, sine, rel, conv_x, conv_bc)


def solution(mesh):
    chips = Mesh(mesh.devices.reshape(SIZES), AXES)
    head = ("yl", "c")
    in_specs = (
        P(AXES, None), P(AXES), P(AXES),
        P(FSDP, head), P(FSDP, head), P(FSDP, head),
        P(None, head), P(),
    )
    out_specs = (P(FSDP, head), P(FSDP, None), P(FSDP, head), P(FSDP, None))
    return jax.shard_map(shards, mesh=chips, in_specs=in_specs, out_specs=out_specs, check_vma=False)
```

```python
import jax
import jax.numpy as jnp
from jax import lax
from jax.experimental import pallas as pl
from jax.experimental.pallas import tpu as pltpu
from jax.sharding import Mesh, PartitionSpec as P

HD = 128
HALO = 16
rope_base = 10000.0

AXES = ("zh", "zl", "yh", "x", "yl", "c")
SIZES = (4, 4, 2, 4, 4, 2)
FSDP = AXES[:4]


def permute_kernel(tokens_ref, extra_ref, out_ref, stack_ref):
    for p in range(8):
        stack_ref[p * 32 : (p + 1) * 32, :] = tokens_ref[:, p * 640 : (p + 1) * 640]
    source = lax.broadcasted_iota(jnp.int32, (640, 640), 0)
    target = lax.broadcasted_iota(jnp.int32, (640, 640), 1)
    wanted = target // 40 % 4 * 160 + target // 160 * 40 + target % 40
    pick = jnp.where(source == wanted, 1.0, 0.0).astype(jnp.bfloat16)
    moved = jnp.dot(stack_ref[...], pick, preferred_element_type=jnp.float32)
    for x in range(4):
        piece = jnp.concatenate(
            [moved[p * 32 : (p + 1) * 32, x * 160 : (x + 1) * 160] for p in range(8)], axis=1
        ).astype(jnp.bfloat16)
        for yl in range(4):
            out_ref[x * 4 + yl, :, 0:1280] = piece
            out_ref[x * 4 + yl, :, 1280:] = extra_ref[...]


def partial_kernel(core_ref, own_ref, other_ref, *refs):
    tail_ref, w_ref, out_ref = refs if len(refs) == 3 else (None,) + refs
    core = core_ref[0]
    width, columns = w_ref.shape
    lead = 0 if tail_ref is None else HALO
    for first in range(0, columns, 256):
        cols = slice(first, min(first + 256, columns))
        for mine in (True, False):
            rows = (own_ref if mine else other_ref)[:, 0:width]
            if lead and not mine:
                rows = jnp.concatenate([rows, tail_ref[...]], axis=0)
            part = jnp.dot(rows, w_ref[:, cols], preferred_element_type=jnp.float32).astype(jnp.bfloat16)
            place = core if mine else 1 - core
            for x in range(4):
                for yl in range(4):
                    at = pl.multiple_of(lead + yl * 64 + place * 32, 16)
                    out_ref[x, pl.ds(at, 32), cols] = part[(x * 4 + yl) * 32 : (x * 4 + yl + 1) * 32]
            if lead and not mine:
                out_ref[0, 0:HALO, cols] = part[512 : 512 + HALO]
    if lead:
        for x in range(3):
            out_ref[x + 1, 0:HALO, :] = out_ref[x, 256 : 256 + HALO, :]


def final_kernel(
    qparts_ref, xs_ref, s_ref, cos_ref, sin_ref, rel_ref, tx_ref, tbc_ref, q_ref, k_ref, x_ref, bc_ref, ext_ref
):
    rows = q_ref.shape[0]
    cosine = cos_ref[...]
    sine = sin_ref[...]

    def turned(values):
        values = values.astype(jnp.float32)
        return (values * cosine + pltpu.roll(values, HD // 2, 1) * sine).astype(jnp.bfloat16)

    def convolved(taps_ref, cols):
        taps = taps_ref[:, cols]
        total = ext_ref[pl.ds(HALO, rows), :] * taps[0:1]
        for step_back in range(1, 4):
            window = ext_ref[pl.ds(HALO - step_back, rows), :] * taps[step_back : step_back + 1]
            total = total + jnp.where(rel_ref[...] >= step_back, window, 0.0)
        return (total / (1.0 + jnp.exp(-total))).astype(jnp.bfloat16)

    for block in range(2):
        cols = slice(block * HD, (block + 1) * HD)
        total = qparts_ref[0, :, cols].astype(jnp.float32)
        for x in range(1, 4):
            total = total + qparts_ref[x, :, cols].astype(jnp.float32)
        q_ref[:, cols] = turned(total.astype(jnp.bfloat16))
        ext_ref[...] = xs_ref[:, cols].astype(jnp.float32)
        x_ref[:, cols] = convolved(tx_ref, cols)
    for block in range(4):
        cols = slice(block * HD, (block + 1) * HD)
        k_ref[:, cols] = turned(s_ref[block, HALO:, :])
        ext_ref[...] = s_ref[4 + block].astype(jnp.float32)
        bc_ref[:, cols] = convolved(tbc_ref, cols)


def shards(tokens, positions, offsets, q_weight, x_weight, shared_weight, conv_x, conv_bc):
    bf16 = jnp.bfloat16
    rows, width = tokens.shape
    quarter = width // 4
    group_rows = 8 * rows
    vmem = pl.BlockSpec(memory_space=pltpu.VMEM)
    smem = pl.BlockSpec(memory_space=pltpu.SMEM)
    params = pltpu.CompilerParams(vmem_limit_bytes=40 * 2**20)
    core = lax.axis_index("c").astype(jnp.int32)
    z = ("zh", "zl")

    weight = jnp.concatenate([q_weight, x_weight, shared_weight], axis=1)
    partner = lax.ppermute(weight, "yh", [(0, 1), (1, 0)])

    extra = jnp.stack([positions >> 8, positions & 255, offsets >> 8, offsets & 255], axis=1)
    extra = jnp.pad(extra, ((0, 0), (0, HD - 4))).astype(bf16)
    split = pl.pallas_call(
        permute_kernel,
        out_shape=jax.ShapeDtypeStruct((16, rows, quarter + HD), bf16),
        in_specs=[vmem, vmem],
        out_specs=vmem,
        scratch_shapes=[pltpu.VMEM((8 * rows, width // 8), bf16)],
        compiler_params=params,
        name="permute_columns",
    )(tokens, extra)
    split, partner = lax.optimization_barrier((split, partner))
    own_t = lax.all_to_all(split, ("x", "yl"), 0, 0).reshape(16 * rows, quarter + HD)

    low = lax.axis_index("yh") == 0
    pair = jnp.concatenate([jnp.where(low, weight, partner), jnp.where(low, partner, weight)], axis=0)

    w_xs = lax.all_gather(pair[:, 256:], z, axis=0, tiled=True)
    own_t, w_xs = lax.optimization_barrier((own_t, w_xs))
    other_t = lax.ppermute(own_t, "c", [(0, 1), (1, 0)])
    tail = own_t[16 * rows - HALO :, :quarter]
    sources = [(2 * i + 1, 2 * i + 2) for i in range(31)]
    tail = lax.ppermute(tail, ("zh", "zl", "yh", "c"), sources) + lax.ppermute(
        tail, ("zh", "zl", "yh", "c"), [(source, target + 1) for source, target in sources]
    )

    def partial(name, lead, operands):
        return pl.pallas_call(
            partial_kernel,
            out_shape=jax.ShapeDtypeStruct((4, lead + group_rows, operands[-1].shape[1]), bf16),
            in_specs=[smem] + [vmem] * len(operands),
            out_specs=vmem,
            compiler_params=params,
            name=name,
        )(core.reshape(1), *operands)

    xs_part = partial("partial_xs", HALO, (own_t, other_t, tail, w_xs))
    pair_q, xs_part = lax.optimization_barrier((pair[:, :256], xs_part))
    xs_parts = lax.all_to_all(xs_part, "x", 0, 0)
    w_q = lax.all_gather(pair_q, z, axis=0, tiled=True)
    xs_parts, w_q = lax.optimization_barrier((xs_parts, w_q))
    q_part = partial("partial_q", 0, (own_t, other_t, w_q))
    q_parts = lax.all_to_all(q_part, "x", 0, 0)

    xs = jnp.sum(xs_parts.astype(jnp.float32), axis=0).astype(bf16)
    s_own, _ = lax.optimization_barrier((xs[:, 256:], q_part))
    s_all = lax.all_gather(s_own, ("yl", "c"), axis=0)
    q_parts, s_all = lax.optimization_barrier((q_parts, s_all))

    at = lax.axis_index("x") * (4 * rows)
    near = lax.dynamic_slice(own_t, (at, quarter), (4 * rows, HD)).reshape(4, 1, rows, HD)
    far = lax.dynamic_slice(other_t, (at, quarter), (4 * rows, HD)).reshape(4, 1, rows, HD)
    first = jnp.where(core == 0, near, far)
    second = jnp.where(core == 0, far, near)
    places = jnp.concatenate([first, second], axis=1).reshape(group_rows, HD)[:, :4].astype(jnp.float32)
    half = HD // 2
    index = jnp.arange(half, dtype=jnp.float32)
    inverse = jnp.exp(-jnp.log(jnp.float32(rope_base)) * index / jnp.float32(half))
    angle = (places[:, 0] * 256.0 + places[:, 1])[:, None] * inverse[None, :]
    cosine, sine = jnp.cos(angle), jnp.sin(angle)
    cosine = jnp.concatenate([cosine, cosine], axis=1)
    sine = jnp.concatenate([-sine, sine], axis=1)
    starts = (places[:, 2] * 256.0 + places[:, 3]).astype(jnp.int32)
    row_ids = lax.axis_index(FSDP) * group_rows + jnp.arange(group_rows, dtype=jnp.int32)
    rel = jnp.broadcast_to((row_ids - starts)[:, None], (group_rows, HD))

    return pl.pallas_call(
        final_kernel,
        out_shape=(
            jax.ShapeDtypeStruct((group_rows, 256), bf16),
            jax.ShapeDtypeStruct((group_rows, 512), bf16),
            jax.ShapeDtypeStruct((group_rows, 256), bf16),
            jax.ShapeDtypeStruct((group_rows, 512), bf16),
        ),
        in_specs=[vmem] * 8,
        out_specs=(vmem,) * 4,
        scratch_shapes=[pltpu.VMEM((group_rows + HALO, HD), jnp.float32)],
        compiler_params=params,
        name="rotate_and_convolve",
    )(q_parts, xs, s_all, cosine, sine, rel, conv_x, conv_bc)


def solution(mesh):
    chips = Mesh(mesh.devices.reshape(SIZES), AXES)
    head = ("yl", "c")
    in_specs = (
        P(AXES, None), P(AXES), P(AXES),
        P(FSDP, head), P(FSDP, head), P(FSDP, head),
        P(None, head), P(),
    )
    out_specs = (P(FSDP, head), P(FSDP, None), P(FSDP, head), P(FSDP, None))
    return jax.shard_map(shards, mesh=chips, in_specs=in_specs, out_specs=out_specs, check_vma=False)
```

```python
import functools

import jax
import jax.numpy as jnp
from jax import lax
from jax.experimental import pallas as pl
from jax.experimental.pallas import tpu as pltpu
from jax.sharding import Mesh, PartitionSpec as P

HD = 128
HALO = 16
rope_base = 10000.0

AXES = ("zh", "zl", "yh", "x", "yl", "c")
SIZES = (4, 4, 2, 4, 4, 2)
FSDP = AXES[:4]


def permute_kernel(tokens_ref, extra_ref, out_ref, stack_ref):
    for p in range(8):
        stack_ref[p * 32 : (p + 1) * 32, :] = tokens_ref[:, p * 640 : (p + 1) * 640]
    source = lax.broadcasted_iota(jnp.int32, (640, 640), 0)
    target = lax.broadcasted_iota(jnp.int32, (640, 640), 1)
    wanted = target // 40 % 2 * 320 + target // 80 % 2 * 160 + target // 160 * 40 + target % 40
    pick = jnp.where(source == wanted, 1.0, 0.0).astype(jnp.bfloat16)
    moved = jnp.dot(stack_ref[...], pick, preferred_element_type=jnp.float32)
    for x in range(4):
        piece = jnp.concatenate(
            [
                moved[p * 32 : (p + 1) * 32, x * 160 + yh * 80 : x * 160 + (yh + 1) * 80]
                for yh in range(2)
                for p in range(8)
            ],
            axis=1,
        ).astype(jnp.bfloat16)
        for yl in range(4):
            out_ref[x * 4 + yl, :, 0:1280] = piece
            out_ref[x * 4 + yl, :, 1280:] = extra_ref[...]


def partial_kernel(first, place_ref, own_ref, other_ref, tail_ref, w_own_ref, w_other_ref, out_ref):
    core, yh = place_ref[0], place_ref[1]
    half = w_own_ref.shape[0]
    near = pl.ds(pl.multiple_of(yh * half, 128), half)
    far = pl.ds(pl.multiple_of((1 - yh) * half, 128), half)
    columns = out_ref.shape[2]
    for start in range(0, columns, 256):
        cols = slice(start, min(start + 256, columns))
        w_cols = slice(first + cols.start, first + cols.stop)
        for mine in (True, False):
            part = 0.0
            for at_k, w_ref in ((near, w_own_ref), (far, w_other_ref)):
                rows = (own_ref if mine else other_ref)[:, at_k]
                if not mine:
                    rows = jnp.concatenate([rows, tail_ref[:, at_k]], axis=0)
                part = part + jnp.dot(rows, w_ref[:, w_cols], preferred_element_type=jnp.float32)
            part = part.astype(jnp.bfloat16)
            place = core if mine else 1 - core
            for x in range(4):
                for yl in range(4):
                    at = pl.multiple_of(HALO + yl * 64 + place * 32, 16)
                    out_ref[x, pl.ds(at, 32), cols] = part[(x * 4 + yl) * 32 : (x * 4 + yl + 1) * 32]
            if not mine:
                out_ref[0, 0:HALO, cols] = part[512 : 512 + HALO]
    for x in range(3):
        out_ref[x + 1, 0:HALO, :] = out_ref[x, 256 : 256 + HALO, :]


def final_kernel(
    parts_ref, s_ref, cos_ref, sin_ref, rel_ref, tx_ref, tbc_ref, q_ref, k_ref, x_ref, bc_ref, ext_ref
):
    rows = q_ref.shape[0]
    cosine = cos_ref[...]
    sine = sin_ref[...]

    def turned(values):
        values = values.astype(jnp.float32)
        return (values * cosine + pltpu.roll(values, HD // 2, 1) * sine).astype(jnp.bfloat16)

    def convolved(taps_ref, cols):
        taps = taps_ref[:, cols]
        total = ext_ref[pl.ds(HALO, rows), :] * taps[0:1]
        for step_back in range(1, 4):
            window = ext_ref[pl.ds(HALO - step_back, rows), :] * taps[step_back : step_back + 1]
            total = total + jnp.where(rel_ref[...] >= step_back, window, 0.0)
        return (total / (1.0 + jnp.exp(-total))).astype(jnp.bfloat16)

    def summed(first, cols):
        total = parts_ref[0, first:, cols].astype(jnp.float32)
        for x in range(1, 4):
            total = total + parts_ref[x, first:, cols].astype(jnp.float32)
        return total.astype(jnp.bfloat16)

    for block in range(2):
        cols = slice(block * HD, (block + 1) * HD)
        q_ref[:, cols] = turned(summed(HALO, cols))
        ext_ref[...] = summed(0, slice(256 + block * HD, 256 + (block + 1) * HD)).astype(jnp.float32)
        x_ref[:, cols] = convolved(tx_ref, cols)
    for block in range(4):
        cols = slice(block * HD, (block + 1) * HD)
        k_ref[:, cols] = turned(s_ref[block, HALO:, :])
        ext_ref[...] = s_ref[4 + block].astype(jnp.float32)
        bc_ref[:, cols] = convolved(tbc_ref, cols)


def shards(tokens, positions, offsets, q_weight, x_weight, shared_weight, conv_x, conv_bc):
    bf16 = jnp.bfloat16
    rows, width = tokens.shape
    quarter = width // 4
    group_rows = 8 * rows
    vmem = pl.BlockSpec(memory_space=pltpu.VMEM)
    smem = pl.BlockSpec(memory_space=pltpu.SMEM)
    params = pltpu.CompilerParams(vmem_limit_bytes=40 * 2**20)
    core = lax.axis_index("c").astype(jnp.int32)
    z = ("zh", "zl")

    extra = jnp.stack([positions >> 8, positions & 255, offsets >> 8, offsets & 255], axis=1)
    extra = jnp.pad(extra, ((0, 0), (0, HD - 4))).astype(bf16)
    split = pl.pallas_call(
        permute_kernel,
        out_shape=jax.ShapeDtypeStruct((16, rows, quarter + HD), bf16),
        in_specs=[vmem, vmem],
        out_specs=vmem,
        scratch_shapes=[pltpu.VMEM((8 * rows, width // 8), bf16)],
        compiler_params=params,
        name="permute_columns",
    )(tokens, extra)
    own_t = lax.all_to_all(split, ("x", "yl"), 0, 0).reshape(16 * rows, quarter + HD)

    weight = jnp.concatenate([q_weight, x_weight, shared_weight], axis=1)
    partner = lax.ppermute(weight, "yh", [(0, 1), (1, 0)])
    w_own = lax.all_gather(weight, z, axis=0, tiled=True)
    own_t, w_own, partner = lax.optimization_barrier((own_t, w_own, partner))
    other_t = lax.ppermute(own_t, "c", [(0, 1), (1, 0)])
    tail = own_t[16 * rows - HALO :, :quarter]
    sources = [(2 * i + 1, 2 * i + 2) for i in range(31)]
    tail = lax.ppermute(tail, ("zh", "zl", "yh", "c"), sources) + lax.ppermute(
        tail, ("zh", "zl", "yh", "c"), [(source, target + 1) for source, target in sources]
    )

    w_other = lax.all_gather(partner, z, axis=0, tiled=True)

    place = jnp.stack([core, lax.axis_index("yh").astype(jnp.int32)])

    def partial(name, first, columns, *operands):
        return pl.pallas_call(
            functools.partial(partial_kernel, first),
            out_shape=jax.ShapeDtypeStruct((4, HALO + group_rows, columns), bf16),
            in_specs=[smem] + [vmem] * len(operands),
            out_specs=vmem,
            compiler_params=params,
            name=name,
        )(place, *operands)

    s_part = partial("partial_s", 512, HD, own_t, other_t, tail, w_own, w_other)
    tail, s_part = lax.optimization_barrier((tail, s_part))
    s_parts = lax.all_to_all(s_part, "x", 0, 0)
    qx_part = partial("partial_qx", 0, 512, own_t, other_t, tail, w_own, w_other)
    s_parts, qx_part = lax.optimization_barrier((s_parts, qx_part))
    qx_parts = lax.all_to_all(qx_part, "x", 0, 0)
    s_own = jnp.sum(s_parts.astype(jnp.float32), axis=0).astype(bf16)
    s_all = lax.all_gather(s_own, ("yl", "c"), axis=0)
    qx_parts, s_all = lax.optimization_barrier((qx_parts, s_all))

    at = lax.axis_index("x") * (4 * rows)
    near = lax.dynamic_slice(own_t, (at, quarter), (4 * rows, HD)).reshape(4, 1, rows, HD)
    far = lax.dynamic_slice(other_t, (at, quarter), (4 * rows, HD)).reshape(4, 1, rows, HD)
    first = jnp.where(core == 0, near, far)
    second = jnp.where(core == 0, far, near)
    places = jnp.concatenate([first, second], axis=1).reshape(group_rows, HD)[:, :4].astype(jnp.float32)
    half = HD // 2
    index = jnp.arange(half, dtype=jnp.float32)
    inverse = jnp.exp(-jnp.log(jnp.float32(rope_base)) * index / jnp.float32(half))
    angle = (places[:, 0] * 256.0 + places[:, 1])[:, None] * inverse[None, :]
    cosine, sine = jnp.cos(angle), jnp.sin(angle)
    cosine = jnp.concatenate([cosine, cosine], axis=1)
    sine = jnp.concatenate([-sine, sine], axis=1)
    starts = (places[:, 2] * 256.0 + places[:, 3]).astype(jnp.int32)
    row_ids = lax.axis_index(FSDP) * group_rows + jnp.arange(group_rows, dtype=jnp.int32)
    rel = jnp.broadcast_to((row_ids - starts)[:, None], (group_rows, HD))

    return pl.pallas_call(
        final_kernel,
        out_shape=(
            jax.ShapeDtypeStruct((group_rows, 256), bf16),
            jax.ShapeDtypeStruct((group_rows, 512), bf16),
            jax.ShapeDtypeStruct((group_rows, 256), bf16),
            jax.ShapeDtypeStruct((group_rows, 512), bf16),
        ),
        in_specs=[vmem] * 7,
        out_specs=(vmem,) * 4,
        scratch_shapes=[pltpu.VMEM((group_rows + HALO, HD), jnp.float32)],
        compiler_params=params,
        name="rotate_and_convolve",
    )(qx_parts, s_all, cosine, sine, rel, conv_x, conv_bc)


def solution(mesh):
    chips = Mesh(mesh.devices.reshape(SIZES), AXES)
    head = ("yl", "c")
    in_specs = (
        P(AXES, None), P(AXES), P(AXES),
        P(FSDP, head), P(FSDP, head), P(FSDP, head),
        P(None, head), P(),
    )
    out_specs = (P(FSDP, head), P(FSDP, None), P(FSDP, head), P(FSDP, None))
    return jax.shard_map(shards, mesh=chips, in_specs=in_specs, out_specs=out_specs, check_vma=False)
```

```python
import functools

import jax
import jax.numpy as jnp
from jax import lax
from jax.experimental import pallas as pl
from jax.experimental.pallas import tpu as pltpu
from jax.sharding import Mesh, PartitionSpec as P

HD = 128
HALO = 16
rope_base = 10000.0

AXES = ("zh", "zl", "yh", "x", "yl", "c")
SIZES = (4, 4, 2, 4, 4, 2)
FSDP = AXES[:4]


def permute_kernel(tokens_ref, extra_ref, out_ref, stack_ref):
    for p in range(8):
        stack_ref[p * 32 : (p + 1) * 32, :] = tokens_ref[:, p * 640 : (p + 1) * 640]
    source = lax.broadcasted_iota(jnp.int32, (640, 640), 0)
    target = lax.broadcasted_iota(jnp.int32, (640, 640), 1)
    wanted = target // 40 % 2 * 320 + target // 80 % 2 * 160 + target // 160 * 40 + target % 40
    pick = jnp.where(source == wanted, 1.0, 0.0).astype(jnp.bfloat16)
    moved = jnp.dot(stack_ref[...], pick, preferred_element_type=jnp.float32)
    for x in range(4):
        piece = jnp.concatenate(
            [
                moved[p * 32 : (p + 1) * 32, x * 160 + yh * 80 : x * 160 + (yh + 1) * 80]
                for yh in range(2)
                for p in range(8)
            ],
            axis=1,
        ).astype(jnp.bfloat16)
        for yl in range(4):
            out_ref[x * 4 + yl, :, 0:1280] = piece
            out_ref[x * 4 + yl, :, 1280:] = extra_ref[...]


def partial_kernel(first, place_ref, own_ref, other_ref, tail_ref, w_own_ref, w_other_ref, out_ref):
    core, yh = place_ref[0], place_ref[1]
    half = w_own_ref.shape[0]
    near = pl.ds(pl.multiple_of(yh * half, 128), half)
    far = pl.ds(pl.multiple_of((1 - yh) * half, 128), half)
    columns = out_ref.shape[2]
    for start in range(0, columns, 256):
        cols = slice(start, min(start + 256, columns))
        own_cols = slice(first + cols.start, first + cols.stop)
        for mine in (True, False):
            part = 0.0
            for at_k, w_ref, w_cols in ((near, w_own_ref, own_cols), (far, w_other_ref, cols)):
                rows = (own_ref if mine else other_ref)[:, at_k]
                if not mine:
                    rows = jnp.concatenate([rows, tail_ref[:, at_k]], axis=0)
                part = part + jnp.dot(rows, w_ref[:, w_cols], preferred_element_type=jnp.float32)
            part = part.astype(jnp.bfloat16)
            place = core if mine else 1 - core
            for x in range(4):
                for yl in range(4):
                    at = pl.multiple_of(HALO + yl * 64 + place * 32, 16)
                    out_ref[x, pl.ds(at, 32), cols] = part[(x * 4 + yl) * 32 : (x * 4 + yl + 1) * 32]
            if not mine:
                out_ref[0, 0:HALO, cols] = part[512 : 512 + HALO]
    for x in range(3):
        out_ref[x + 1, 0:HALO, :] = out_ref[x, 256 : 256 + HALO, :]


def final_kernel(
    parts_ref, s_ref, cos_ref, sin_ref, rel_ref, tx_ref, tbc_ref, q_ref, k_ref, x_ref, bc_ref, ext_ref
):
    rows = q_ref.shape[0]
    cosine = cos_ref[...]
    sine = sin_ref[...]

    def turned(values):
        values = values.astype(jnp.float32)
        return (values * cosine + pltpu.roll(values, HD // 2, 1) * sine).astype(jnp.bfloat16)

    def convolved(taps_ref, cols):
        taps = taps_ref[:, cols]
        total = ext_ref[pl.ds(HALO, rows), :] * taps[0:1]
        for step_back in range(1, 4):
            window = ext_ref[pl.ds(HALO - step_back, rows), :] * taps[step_back : step_back + 1]
            total = total + jnp.where(rel_ref[...] >= step_back, window, 0.0)
        return (total / (1.0 + jnp.exp(-total))).astype(jnp.bfloat16)

    def summed(first, cols):
        total = parts_ref[0, first:, cols].astype(jnp.float32)
        for x in range(1, 4):
            total = total + parts_ref[x, first:, cols].astype(jnp.float32)
        return total.astype(jnp.bfloat16)

    for block in range(2):
        cols = slice(block * HD, (block + 1) * HD)
        q_ref[:, cols] = turned(summed(HALO, cols))
        ext_ref[...] = summed(0, slice(256 + block * HD, 256 + (block + 1) * HD)).astype(jnp.float32)
        x_ref[:, cols] = convolved(tx_ref, cols)
    for block in range(4):
        cols = slice(block * HD, (block + 1) * HD)
        k_ref[:, cols] = turned(s_ref[block, HALO:, :])
        ext_ref[...] = s_ref[4 + block].astype(jnp.float32)
        bc_ref[:, cols] = convolved(tbc_ref, cols)


def shards(tokens, positions, offsets, q_weight, x_weight, shared_weight, conv_x, conv_bc):
    bf16 = jnp.bfloat16
    rows, width = tokens.shape
    quarter = width // 4
    group_rows = 8 * rows
    vmem = pl.BlockSpec(memory_space=pltpu.VMEM)
    smem = pl.BlockSpec(memory_space=pltpu.SMEM)
    params = pltpu.CompilerParams(vmem_limit_bytes=40 * 2**20)
    core = lax.axis_index("c").astype(jnp.int32)
    z = ("zh", "zl")

    extra = jnp.stack([positions >> 8, positions & 255, offsets >> 8, offsets & 255], axis=1)
    extra = jnp.pad(extra, ((0, 0), (0, HD - 4))).astype(bf16)
    split = pl.pallas_call(
        permute_kernel,
        out_shape=jax.ShapeDtypeStruct((16, rows, quarter + HD), bf16),
        in_specs=[vmem, vmem],
        out_specs=vmem,
        scratch_shapes=[pltpu.VMEM((8 * rows, width // 8), bf16)],
        compiler_params=params,
        name="permute_columns",
    )(tokens, extra)
    own_t = lax.all_to_all(split, ("x", "yl"), 0, 0).reshape(16 * rows, quarter + HD)

    weight = jnp.concatenate([q_weight, x_weight, shared_weight], axis=1)
    w_own = lax.all_gather(weight, z, axis=0, tiled=True)
    own_t, w_own = lax.optimization_barrier((own_t, w_own))
    swap = [(0, 1), (1, 0)]
    w_other_s = lax.ppermute(w_own[:, 512:], "yh", swap)
    other_t = lax.ppermute(own_t, "c", [(0, 1), (1, 0)])
    tail = own_t[16 * rows - HALO :, :quarter]
    sources = [(2 * i + 1, 2 * i + 2) for i in range(31)]
    tail = lax.ppermute(tail, ("zh", "zl", "yh", "c"), sources) + lax.ppermute(
        tail, ("zh", "zl", "yh", "c"), [(source, target + 1) for source, target in sources]
    )

    w_qx, w_other_s, tail = lax.optimization_barrier((w_own[:, :512], w_other_s, tail))
    w_other_qx = lax.ppermute(w_qx, "yh", swap)

    place = jnp.stack([core, lax.axis_index("yh").astype(jnp.int32)])

    def partial(name, first, columns, *operands):
        return pl.pallas_call(
            functools.partial(partial_kernel, first),
            out_shape=jax.ShapeDtypeStruct((4, HALO + group_rows, columns), bf16),
            in_specs=[smem] + [vmem] * len(operands),
            out_specs=vmem,
            compiler_params=params,
            name=name,
        )(place, *operands)

    s_part = partial("partial_s", 512, HD, own_t, other_t, tail, w_own, w_other_s)
    tail, s_part = lax.optimization_barrier((tail, s_part))
    s_parts = lax.all_to_all(s_part, "x", 0, 0)
    qx_part = partial("partial_qx", 0, 512, own_t, other_t, tail, w_own, w_other_qx)
    s_parts, qx_part = lax.optimization_barrier((s_parts, qx_part))
    qx_parts = lax.all_to_all(qx_part, "x", 0, 0)
    s_own = jnp.sum(s_parts.astype(jnp.float32), axis=0).astype(bf16)
    s_all = lax.all_gather(s_own, ("yl", "c"), axis=0)
    qx_parts, s_all = lax.optimization_barrier((qx_parts, s_all))

    at = lax.axis_index("x") * (4 * rows)
    near = lax.dynamic_slice(own_t, (at, quarter), (4 * rows, HD)).reshape(4, 1, rows, HD)
    far = lax.dynamic_slice(other_t, (at, quarter), (4 * rows, HD)).reshape(4, 1, rows, HD)
    first = jnp.where(core == 0, near, far)
    second = jnp.where(core == 0, far, near)
    places = jnp.concatenate([first, second], axis=1).reshape(group_rows, HD)[:, :4].astype(jnp.float32)
    half = HD // 2
    index = jnp.arange(half, dtype=jnp.float32)
    inverse = jnp.exp(-jnp.log(jnp.float32(rope_base)) * index / jnp.float32(half))
    angle = (places[:, 0] * 256.0 + places[:, 1])[:, None] * inverse[None, :]
    cosine, sine = jnp.cos(angle), jnp.sin(angle)
    cosine = jnp.concatenate([cosine, cosine], axis=1)
    sine = jnp.concatenate([-sine, sine], axis=1)
    starts = (places[:, 2] * 256.0 + places[:, 3]).astype(jnp.int32)
    row_ids = lax.axis_index(FSDP) * group_rows + jnp.arange(group_rows, dtype=jnp.int32)
    rel = jnp.broadcast_to((row_ids - starts)[:, None], (group_rows, HD))

    return pl.pallas_call(
        final_kernel,
        out_shape=(
            jax.ShapeDtypeStruct((group_rows, 256), bf16),
            jax.ShapeDtypeStruct((group_rows, 512), bf16),
            jax.ShapeDtypeStruct((group_rows, 256), bf16),
            jax.ShapeDtypeStruct((group_rows, 512), bf16),
        ),
        in_specs=[vmem] * 7,
        out_specs=(vmem,) * 4,
        scratch_shapes=[pltpu.VMEM((group_rows + HALO, HD), jnp.float32)],
        compiler_params=params,
        name="rotate_and_convolve",
    )(qx_parts, s_all, cosine, sine, rel, conv_x, conv_bc)


def solution(mesh):
    chips = Mesh(mesh.devices.reshape(SIZES), AXES)
    head = ("yl", "c")
    in_specs = (
        P(AXES, None), P(AXES), P(AXES),
        P(FSDP, head), P(FSDP, head), P(FSDP, head),
        P(None, head), P(),
    )
    out_specs = (P(FSDP, head), P(FSDP, None), P(FSDP, head), P(FSDP, None))
    return jax.shard_map(shards, mesh=chips, in_specs=in_specs, out_specs=out_specs, check_vma=False)
```

```python
import functools

import jax
import jax.numpy as jnp
from jax import lax
from jax.experimental import pallas as pl
from jax.experimental.pallas import tpu as pltpu
from jax.sharding import Mesh, PartitionSpec as P

HD = 128
HALO = 16
rope_base = 10000.0

AXES = ("zh", "zl", "yh", "x", "yl", "c")
SIZES = (4, 4, 2, 4, 4, 2)
FSDP = AXES[:4]


def permute_kernel(tokens_ref, extra_ref, out_ref, stack_ref):
    for p in range(8):
        stack_ref[p * 32 : (p + 1) * 32, :] = tokens_ref[:, p * 640 : (p + 1) * 640]
    source = lax.broadcasted_iota(jnp.int32, (640, 640), 0)
    target = lax.broadcasted_iota(jnp.int32, (640, 640), 1)
    wanted = target // 40 % 2 * 320 + target // 80 % 2 * 160 + target // 160 * 40 + target % 40
    pick = jnp.where(source == wanted, 1.0, 0.0).astype(jnp.bfloat16)
    moved = jnp.dot(stack_ref[...], pick, preferred_element_type=jnp.float32)
    for x in range(4):
        piece = jnp.concatenate(
            [
                moved[p * 32 : (p + 1) * 32, x * 160 + yh * 80 : x * 160 + (yh + 1) * 80]
                for yh in range(2)
                for p in range(8)
            ],
            axis=1,
        ).astype(jnp.bfloat16)
        for yl in range(4):
            out_ref[x * 4 + yl, :, 0:1280] = piece
            out_ref[x * 4 + yl, :, 1280:] = extra_ref[...]


def partial_kernel(first, place_ref, own_ref, other_ref, tail_ref, w_own_ref, w_other_ref, out_ref):
    core, yh = place_ref[0], place_ref[1]
    half = w_own_ref.shape[0]
    near = pl.ds(pl.multiple_of(yh * half, 128), half)
    far = pl.ds(pl.multiple_of((1 - yh) * half, 128), half)
    columns = out_ref.shape[2]
    for start in range(0, columns, 256):
        cols = slice(start, min(start + 256, columns))
        own_cols = slice(first + cols.start, first + cols.stop)
        for mine in (True, False):
            part = 0.0
            for at_k, w_ref, w_cols in ((near, w_own_ref, own_cols), (far, w_other_ref, cols)):
                rows = (own_ref if mine else other_ref)[:, at_k]
                if not mine:
                    rows = jnp.concatenate([rows, tail_ref[:, at_k]], axis=0)
                part = part + jnp.dot(rows, w_ref[:, w_cols], preferred_element_type=jnp.float32)
            part = part.astype(jnp.bfloat16)
            place = core if mine else 1 - core
            for x in range(4):
                for yl in range(4):
                    at = pl.multiple_of(HALO + yl * 64 + place * 32, 16)
                    out_ref[x, pl.ds(at, 32), cols] = part[(x * 4 + yl) * 32 : (x * 4 + yl + 1) * 32]
            if not mine:
                out_ref[0, 0:HALO, cols] = part[512 : 512 + HALO]
    for x in range(3):
        out_ref[x + 1, 0:HALO, :] = out_ref[x, 256 : 256 + HALO, :]


def final_kernel(
    q_parts_ref, x_parts_ref, s_ref, cos_ref, sin_ref, rel_ref, tx_ref, tbc_ref, q_ref, k_ref, x_ref, bc_ref, ext_ref
):
    rows = q_ref.shape[0]
    cosine = cos_ref[...]
    sine = sin_ref[...]

    def turned(values):
        values = values.astype(jnp.float32)
        return (values * cosine + pltpu.roll(values, HD // 2, 1) * sine).astype(jnp.bfloat16)

    def convolved(taps_ref, cols):
        taps = taps_ref[:, cols]
        total = ext_ref[pl.ds(HALO, rows), :] * taps[0:1]
        for step_back in range(1, 4):
            window = ext_ref[pl.ds(HALO - step_back, rows), :] * taps[step_back : step_back + 1]
            total = total + jnp.where(rel_ref[...] >= step_back, window, 0.0)
        return (total / (1.0 + jnp.exp(-total))).astype(jnp.bfloat16)

    def summed(parts_ref, first, cols):
        total = parts_ref[0, first:, cols].astype(jnp.float32)
        for x in range(1, 4):
            total = total + parts_ref[x, first:, cols].astype(jnp.float32)
        return total.astype(jnp.bfloat16)

    for block in range(2):
        cols = slice(block * HD, (block + 1) * HD)
        q_ref[:, cols] = turned(summed(q_parts_ref, HALO, cols))
        ext_ref[...] = summed(x_parts_ref, 0, cols).astype(jnp.float32)
        x_ref[:, cols] = convolved(tx_ref, cols)
    for block in range(4):
        cols = slice(block * HD, (block + 1) * HD)
        k_ref[:, cols] = turned(s_ref[block, HALO:, :])
        ext_ref[...] = s_ref[4 + block].astype(jnp.float32)
        bc_ref[:, cols] = convolved(tbc_ref, cols)


def shards(tokens, positions, offsets, q_weight, x_weight, shared_weight, conv_x, conv_bc):
    bf16 = jnp.bfloat16
    rows, width = tokens.shape
    quarter = width // 4
    group_rows = 8 * rows
    vmem = pl.BlockSpec(memory_space=pltpu.VMEM)
    smem = pl.BlockSpec(memory_space=pltpu.SMEM)
    params = pltpu.CompilerParams(vmem_limit_bytes=40 * 2**20)
    core = lax.axis_index("c").astype(jnp.int32)
    z = ("zh", "zl")

    extra = jnp.stack([positions >> 8, positions & 255, offsets >> 8, offsets & 255], axis=1)
    extra = jnp.pad(extra, ((0, 0), (0, HD - 4))).astype(bf16)
    split = pl.pallas_call(
        permute_kernel,
        out_shape=jax.ShapeDtypeStruct((16, rows, quarter + HD), bf16),
        in_specs=[vmem, vmem],
        out_specs=vmem,
        scratch_shapes=[pltpu.VMEM((8 * rows, width // 8), bf16)],
        compiler_params=params,
        name="permute_columns",
    )(tokens, extra)
    own_t = lax.all_to_all(split, ("x", "yl"), 0, 0).reshape(16 * rows, quarter + HD)

    weight = jnp.concatenate([q_weight, x_weight, shared_weight], axis=1)
    w_own = lax.all_gather(weight, z, axis=0, tiled=True)
    own_t, w_own = lax.optimization_barrier((own_t, w_own))
    swap = [(0, 1), (1, 0)]
    w_other_s = lax.ppermute(w_own[:, 512:], "yh", swap)
    other_t = lax.ppermute(own_t, "c", [(0, 1), (1, 0)])
    tail = own_t[16 * rows - HALO :, :quarter]
    sources = [(2 * i + 1, 2 * i + 2) for i in range(31)]
    tail = lax.ppermute(tail, ("zh", "zl", "yh", "c"), sources) + lax.ppermute(
        tail, ("zh", "zl", "yh", "c"), [(source, target + 1) for source, target in sources]
    )

    w_x, w_other_s, tail = lax.optimization_barrier((w_own[:, 256:512], w_other_s, tail))
    w_other_x = lax.ppermute(w_x, "yh", swap)

    place = jnp.stack([core, lax.axis_index("yh").astype(jnp.int32)])

    def partial(name, first, columns, *operands):
        return pl.pallas_call(
            functools.partial(partial_kernel, first),
            out_shape=jax.ShapeDtypeStruct((4, HALO + group_rows, columns), bf16),
            in_specs=[smem] + [vmem] * len(operands),
            out_specs=vmem,
            compiler_params=params,
            name=name,
        )(place, *operands)

    s_part = partial("partial_s", 512, HD, own_t, other_t, tail, w_own, w_other_s)
    s_parts = lax.all_to_all(s_part, "x", 0, 0)
    tail, _, w_q, w_other_x = lax.optimization_barrier((tail, s_part, w_own[:, :256], w_other_x))
    w_other_q = lax.ppermute(w_q, "yh", swap)
    x_part = partial("partial_x", 256, 256, own_t, other_t, tail, w_own, w_other_x)
    s_parts, x_part = lax.optimization_barrier((s_parts, x_part))
    x_parts = lax.all_to_all(x_part, "x", 0, 0)
    s_own = jnp.sum(s_parts.astype(jnp.float32), axis=0).astype(bf16)
    s_all = lax.all_gather(s_own, ("yl", "c"), axis=0)
    x_parts, w_other_q, s_all = lax.optimization_barrier((x_parts, w_other_q, s_all))
    q_part = partial("partial_q", 0, 256, own_t, other_t, tail, w_own, w_other_q)
    q_parts = lax.all_to_all(q_part, "x", 0, 0)

    at = lax.axis_index("x") * (4 * rows)
    near = lax.dynamic_slice(own_t, (at, quarter), (4 * rows, HD)).reshape(4, 1, rows, HD)
    far = lax.dynamic_slice(other_t, (at, quarter), (4 * rows, HD)).reshape(4, 1, rows, HD)
    first = jnp.where(core == 0, near, far)
    second = jnp.where(core == 0, far, near)
    places = jnp.concatenate([first, second], axis=1).reshape(group_rows, HD)[:, :4].astype(jnp.float32)
    half = HD // 2
    index = jnp.arange(half, dtype=jnp.float32)
    inverse = jnp.exp(-jnp.log(jnp.float32(rope_base)) * index / jnp.float32(half))
    angle = (places[:, 0] * 256.0 + places[:, 1])[:, None] * inverse[None, :]
    cosine, sine = jnp.cos(angle), jnp.sin(angle)
    cosine = jnp.concatenate([cosine, cosine], axis=1)
    sine = jnp.concatenate([-sine, sine], axis=1)
    starts = (places[:, 2] * 256.0 + places[:, 3]).astype(jnp.int32)
    row_ids = lax.axis_index(FSDP) * group_rows + jnp.arange(group_rows, dtype=jnp.int32)
    rel = jnp.broadcast_to((row_ids - starts)[:, None], (group_rows, HD))

    return pl.pallas_call(
        final_kernel,
        out_shape=(
            jax.ShapeDtypeStruct((group_rows, 256), bf16),
            jax.ShapeDtypeStruct((group_rows, 512), bf16),
            jax.ShapeDtypeStruct((group_rows, 256), bf16),
            jax.ShapeDtypeStruct((group_rows, 512), bf16),
        ),
        in_specs=[vmem] * 8,
        out_specs=(vmem,) * 4,
        scratch_shapes=[pltpu.VMEM((group_rows + HALO, HD), jnp.float32)],
        compiler_params=params,
        name="rotate_and_convolve",
    )(q_parts, x_parts, s_all, cosine, sine, rel, conv_x, conv_bc)


def solution(mesh):
    chips = Mesh(mesh.devices.reshape(SIZES), AXES)
    head = ("yl", "c")
    in_specs = (
        P(AXES, None), P(AXES), P(AXES),
        P(FSDP, head), P(FSDP, head), P(FSDP, head),
        P(None, head), P(),
    )
    out_specs = (P(FSDP, head), P(FSDP, None), P(FSDP, head), P(FSDP, None))
    return jax.shard_map(shards, mesh=chips, in_specs=in_specs, out_specs=out_specs, check_vma=False)
```

```python
import functools

import jax
import jax.numpy as jnp
from jax import lax
from jax.experimental import pallas as pl
from jax.experimental.pallas import tpu as pltpu
from jax.sharding import Mesh, PartitionSpec as P

HD = 128
HALO = 16
rope_base = 10000.0

AXES = ("zh", "zl", "yh", "x", "yl", "c")
SIZES = (4, 4, 2, 4, 4, 2)
FSDP = AXES[:4]


def permute_kernel(tokens_ref, out_ref, stack_ref):
    for p in range(8):
        stack_ref[p * 32 : (p + 1) * 32, :] = tokens_ref[:, p * 640 : (p + 1) * 640]
    source = lax.broadcasted_iota(jnp.int32, (640, 640), 0)
    target = lax.broadcasted_iota(jnp.int32, (640, 640), 1)
    wanted = target // 40 % 2 * 320 + target // 80 % 2 * 160 + target // 160 * 40 + target % 40
    pick = jnp.where(source == wanted, 1.0, 0.0).astype(jnp.bfloat16)
    moved = jnp.dot(stack_ref[...], pick, preferred_element_type=jnp.float32)
    for x in range(4):
        piece = jnp.concatenate(
            [
                moved[p * 32 : (p + 1) * 32, x * 160 + yh * 80 : x * 160 + (yh + 1) * 80]
                for yh in range(2)
                for p in range(8)
            ],
            axis=1,
        ).astype(jnp.bfloat16)
        for yl in range(4):
            out_ref[x * 4 + yl] = piece


def partial_kernel(first, place_ref, own_ref, other_ref, tail_ref, w_own_ref, w_other_ref, out_ref):
    core, yh = place_ref[0], place_ref[1]
    half = w_own_ref.shape[0]
    near = pl.ds(pl.multiple_of(yh * half, 128), half)
    far = pl.ds(pl.multiple_of((1 - yh) * half, 128), half)
    columns = out_ref.shape[2]
    for start in range(0, columns, 256):
        cols = slice(start, min(start + 256, columns))
        w_cols = slice(first + cols.start, first + cols.stop)
        for mine in (True, False):
            part = 0.0
            for at_k, w_ref in ((near, w_own_ref), (far, w_other_ref)):
                rows = (own_ref if mine else other_ref)[:, at_k]
                if not mine:
                    rows = jnp.concatenate([rows, tail_ref[:, at_k]], axis=0)
                part = part + jnp.dot(rows, w_ref[:, w_cols], preferred_element_type=jnp.float32)
            part = part.astype(jnp.bfloat16)
            place = core if mine else 1 - core
            for x in range(4):
                for yl in range(4):
                    at = pl.multiple_of(HALO + yl * 64 + place * 32, 16)
                    out_ref[x, pl.ds(at, 32), cols] = part[(x * 4 + yl) * 32 : (x * 4 + yl + 1) * 32]
            if not mine:
                out_ref[0, 0:HALO, cols] = part[512 : 512 + HALO]
    for x in range(3):
        out_ref[x + 1, 0:HALO, :] = out_ref[x, 256 : 256 + HALO, :]


def final_kernel(
    parts_ref, s_ref, cos_ref, sin_ref, rel_ref, tx_ref, tbc_ref, q_ref, k_ref, x_ref, bc_ref, ext_ref
):
    rows = q_ref.shape[0]
    cosine = cos_ref[...]
    sine = sin_ref[...]

    def turned(values):
        values = values.astype(jnp.float32)
        return (values * cosine + pltpu.roll(values, HD // 2, 1) * sine).astype(jnp.bfloat16)

    def convolved(taps_ref, cols):
        taps = taps_ref[:, cols]
        total = ext_ref[pl.ds(HALO, rows), :] * taps[0:1]
        for step_back in range(1, 4):
            window = ext_ref[pl.ds(HALO - step_back, rows), :] * taps[step_back : step_back + 1]
            total = total + jnp.where(rel_ref[...] >= step_back, window, 0.0)
        return (total / (1.0 + jnp.exp(-total))).astype(jnp.bfloat16)

    def summed(first, cols):
        total = parts_ref[0, first:, cols].astype(jnp.float32)
        for x in range(1, 4):
            total = total + parts_ref[x, first:, cols].astype(jnp.float32)
        return total.astype(jnp.bfloat16)

    for block in range(2):
        cols = slice(block * HD, (block + 1) * HD)
        q_ref[:, cols] = turned(summed(HALO, cols))
        ext_ref[...] = summed(0, slice(256 + block * HD, 256 + (block + 1) * HD)).astype(jnp.float32)
        x_ref[:, cols] = convolved(tx_ref, cols)
    for block in range(4):
        cols = slice(block * HD, (block + 1) * HD)
        k_ref[:, cols] = turned(s_ref[block, HALO : HALO + rows, :])
        ext_ref[...] = s_ref[4 + block, 0 : HALO + rows, :].astype(jnp.float32)
        bc_ref[:, cols] = convolved(tbc_ref, cols)


def shards(tokens, positions, offsets, q_weight, x_weight, shared_weight, conv_x, conv_bc):
    bf16 = jnp.bfloat16
    rows, width = tokens.shape
    quarter = width // 4
    group_rows = 8 * rows
    vmem = pl.BlockSpec(memory_space=pltpu.VMEM)
    smem = pl.BlockSpec(memory_space=pltpu.SMEM)
    params = pltpu.CompilerParams(vmem_limit_bytes=40 * 2**20)
    core = lax.axis_index("c").astype(jnp.int32)
    z = ("zh", "zl")

    split = pl.pallas_call(
        permute_kernel,
        out_shape=jax.ShapeDtypeStruct((16, rows, quarter), bf16),
        in_specs=[vmem],
        out_specs=vmem,
        scratch_shapes=[pltpu.VMEM((8 * rows, width // 8), bf16)],
        compiler_params=params,
        name="permute_columns",
    )(tokens)
    own_t = lax.all_to_all(split, ("x", "yl"), 0, 0).reshape(16 * rows, quarter)

    weight = jnp.concatenate([q_weight, x_weight, shared_weight], axis=1)
    partner = lax.ppermute(weight, "yh", [(0, 1), (1, 0)])
    w_own = lax.all_gather(weight, z, axis=0, tiled=True)
    own_t, w_own, partner = lax.optimization_barrier((own_t, w_own, partner))
    other_t = lax.ppermute(own_t, "c", [(0, 1), (1, 0)])
    tail = own_t[16 * rows - HALO :]
    sources = [(2 * i + 1, 2 * i + 2) for i in range(31)]
    tail = lax.ppermute(tail, ("zh", "zl", "yh", "c"), sources) + lax.ppermute(
        tail, ("zh", "zl", "yh", "c"), [(source, target + 1) for source, target in sources]
    )

    w_other = lax.all_gather(partner, z, axis=0, tiled=True)

    place = jnp.stack([core, lax.axis_index("yh").astype(jnp.int32)])

    def partial(name, first, columns, *operands):
        return pl.pallas_call(
            functools.partial(partial_kernel, first),
            out_shape=jax.ShapeDtypeStruct((4, HALO + group_rows, columns), bf16),
            in_specs=[smem] + [vmem] * len(operands),
            out_specs=vmem,
            compiler_params=params,
            name=name,
        )(place, *operands)

    s_part = partial("partial_s", 512, HD, own_t, other_t, tail, w_own, w_other)
    tail, s_part = lax.optimization_barrier((tail, s_part))
    s_parts = lax.all_to_all(s_part, "x", 0, 0)
    qx_part = partial("partial_qx", 0, 512, own_t, other_t, tail, w_own, w_other)
    s_parts, qx_part = lax.optimization_barrier((s_parts, qx_part))
    qx_parts = lax.all_to_all(qx_part, "x", 0, 0)
    s_own = jnp.sum(s_parts.astype(jnp.float32), axis=0).astype(bf16)
    extra = jnp.stack([positions >> 8, positions & 255, offsets >> 8, offsets & 255], axis=1)
    extra = jnp.pad(extra, ((0, 0), (0, HD - 4))).astype(bf16)
    s_all = lax.all_gather(jnp.concatenate([s_own, extra], axis=0), ("yl", "c"), axis=0)
    qx_parts, s_all = lax.optimization_barrier((qx_parts, s_all))

    places = s_all[:, HALO + group_rows :, :4].reshape(group_rows, 4).astype(jnp.float32)
    half = HD // 2
    index = jnp.arange(half, dtype=jnp.float32)
    inverse = jnp.exp(-jnp.log(jnp.float32(rope_base)) * index / jnp.float32(half))
    angle = (places[:, 0] * 256.0 + places[:, 1])[:, None] * inverse[None, :]
    cosine, sine = jnp.cos(angle), jnp.sin(angle)
    cosine = jnp.concatenate([cosine, cosine], axis=1)
    sine = jnp.concatenate([-sine, sine], axis=1)
    starts = (places[:, 2] * 256.0 + places[:, 3]).astype(jnp.int32)
    row_ids = lax.axis_index(FSDP) * group_rows + jnp.arange(group_rows, dtype=jnp.int32)
    rel = jnp.broadcast_to((row_ids - starts)[:, None], (group_rows, HD))

    return pl.pallas_call(
        final_kernel,
        out_shape=(
            jax.ShapeDtypeStruct((group_rows, 256), bf16),
            jax.ShapeDtypeStruct((group_rows, 512), bf16),
            jax.ShapeDtypeStruct((group_rows, 256), bf16),
            jax.ShapeDtypeStruct((group_rows, 512), bf16),
        ),
        in_specs=[vmem] * 7,
        out_specs=(vmem,) * 4,
        scratch_shapes=[pltpu.VMEM((group_rows + HALO, HD), jnp.float32)],
        compiler_params=params,
        name="rotate_and_convolve",
    )(qx_parts, s_all, cosine, sine, rel, conv_x, conv_bc)


def solution(mesh):
    chips = Mesh(mesh.devices.reshape(SIZES), AXES)
    head = ("yl", "c")
    in_specs = (
        P(AXES, None), P(AXES), P(AXES),
        P(FSDP, head), P(FSDP, head), P(FSDP, head),
        P(None, head), P(),
    )
    out_specs = (P(FSDP, head), P(FSDP, None), P(FSDP, head), P(FSDP, None))
    return jax.shard_map(shards, mesh=chips, in_specs=in_specs, out_specs=out_specs, check_vma=False)
```

```python
import functools

import jax
import jax.numpy as jnp
from jax import lax
from jax.experimental import pallas as pl
from jax.experimental.pallas import tpu as pltpu
from jax.sharding import Mesh, PartitionSpec as P

HD = 128
HALO = 16
rope_base = 10000.0

AXES = ("zh", "zl", "yh", "x", "yl", "c")
SIZES = (4, 4, 2, 4, 4, 2)
FSDP = AXES[:4]


def permute_kernel(tokens_ref, out_ref, stack_ref):
    for p in range(8):
        stack_ref[p * 32 : (p + 1) * 32, :] = tokens_ref[:, p * 640 : (p + 1) * 640]
    source = lax.broadcasted_iota(jnp.int32, (640, 640), 0)
    target = lax.broadcasted_iota(jnp.int32, (640, 640), 1)
    wanted = target // 40 % 2 * 320 + target // 80 % 2 * 160 + target // 160 * 40 + target % 40
    pick = jnp.where(source == wanted, 1.0, 0.0).astype(jnp.bfloat16)
    moved = jnp.dot(stack_ref[...], pick, preferred_element_type=jnp.float32)
    for x in range(4):
        piece = jnp.concatenate(
            [
                moved[p * 32 : (p + 1) * 32, x * 160 + yh * 80 : x * 160 + (yh + 1) * 80]
                for yh in range(2)
                for p in range(8)
            ],
            axis=1,
        ).astype(jnp.bfloat16)
        for yl in range(4):
            out_ref[x * 4 + yl] = piece


def partial_kernel(first, place_ref, own_ref, other_ref, tail_ref, w_own_ref, w_other_ref, out_ref):
    core, yh = place_ref[0], place_ref[1]
    half = w_own_ref.shape[0]
    near = pl.ds(pl.multiple_of(yh * half, 128), half)
    far = pl.ds(pl.multiple_of((1 - yh) * half, 128), half)
    columns = out_ref.shape[2]
    for start in range(0, columns, 256):
        cols = slice(start, min(start + 256, columns))
        own_cols = slice(first + cols.start, first + cols.stop)
        for rows_ref, place in ((own_ref, core), (other_ref, 1 - core), (tail_ref, None)):
            part = jnp.dot(rows_ref[:, near], w_own_ref[:, own_cols], preferred_element_type=jnp.float32)
            part = part + jnp.dot(rows_ref[:, far], w_other_ref[:, own_cols], preferred_element_type=jnp.float32)
            part = part.astype(jnp.bfloat16)
            if place is None:
                out_ref[0, 0:HALO, cols] = part
                continue
            for x in range(4):
                for yl in range(4):
                    at = pl.multiple_of(HALO + yl * 64 + place * 32, 16)
                    out_ref[x, pl.ds(at, 32), cols] = part[(x * 4 + yl) * 32 : (x * 4 + yl + 1) * 32]
    for x in range(3):
        out_ref[x + 1, 0:HALO, :] = out_ref[x, 256 : 256 + HALO, :]


def final_kernel(
    parts_ref, s_ref, cos_ref, sin_ref, rel_ref, tx_ref, tbc_ref, q_ref, k_ref, x_ref, bc_ref, ext_ref
):
    rows = q_ref.shape[0]
    cosine = cos_ref[...]
    sine = sin_ref[...]

    def turned(values):
        values = values.astype(jnp.float32)
        return (values * cosine + pltpu.roll(values, HD // 2, 1) * sine).astype(jnp.bfloat16)

    def convolved(taps_ref, cols):
        taps = taps_ref[:, cols]
        total = ext_ref[pl.ds(HALO, rows), :] * taps[0:1]
        for step_back in range(1, 4):
            window = ext_ref[pl.ds(HALO - step_back, rows), :] * taps[step_back : step_back + 1]
            total = total + jnp.where(rel_ref[...] >= step_back, window, 0.0)
        return (total / (1.0 + jnp.exp(-total))).astype(jnp.bfloat16)

    def summed(first, cols):
        total = parts_ref[0, first:, cols].astype(jnp.float32)
        for x in range(1, 4):
            total = total + parts_ref[x, first:, cols].astype(jnp.float32)
        return total.astype(jnp.bfloat16)

    for block in range(2):
        cols = slice(block * HD, (block + 1) * HD)
        q_ref[:, cols] = turned(summed(HALO, cols))
        ext_ref[...] = summed(0, slice(256 + block * HD, 256 + (block + 1) * HD)).astype(jnp.float32)
        x_ref[:, cols] = convolved(tx_ref, cols)
    for block in range(4):
        cols = slice(block * HD, (block + 1) * HD)
        k_ref[:, cols] = turned(s_ref[block, HALO : HALO + rows, :])
        ext_ref[...] = s_ref[4 + block, 0 : HALO + rows, :].astype(jnp.float32)
        bc_ref[:, cols] = convolved(tbc_ref, cols)


def shards(tokens, positions, offsets, q_weight, x_weight, shared_weight, conv_x, conv_bc):
    bf16 = jnp.bfloat16
    rows, width = tokens.shape
    quarter = width // 4
    group_rows = 8 * rows
    vmem = pl.BlockSpec(memory_space=pltpu.VMEM)
    smem = pl.BlockSpec(memory_space=pltpu.SMEM)
    params = pltpu.CompilerParams(vmem_limit_bytes=40 * 2**20)
    core = lax.axis_index("c").astype(jnp.int32)
    z = ("zh", "zl")

    split = pl.pallas_call(
        permute_kernel,
        out_shape=jax.ShapeDtypeStruct((16, rows, quarter), bf16),
        in_specs=[vmem],
        out_specs=vmem,
        scratch_shapes=[pltpu.VMEM((8 * rows, width // 8), bf16)],
        compiler_params=params,
        name="permute_columns",
    )(tokens)
    own_t = lax.all_to_all(split, ("x", "yl"), 0, 0).reshape(16 * rows, quarter)

    weight = jnp.concatenate([q_weight, x_weight, shared_weight], axis=1)
    partner = lax.ppermute(weight, "yh", [(0, 1), (1, 0)])
    w_own = lax.all_gather(weight, z, axis=0, tiled=True)
    own_t, w_own, partner = lax.optimization_barrier((own_t, w_own, partner))
    other_t = lax.ppermute(own_t, "c", [(0, 1), (1, 0)])
    tail = own_t[16 * rows - HALO :]
    sources = [(2 * i + 1, 2 * i + 2) for i in range(31)]
    tail = lax.ppermute(tail, ("zh", "zl", "yh", "c"), sources) + lax.ppermute(
        tail, ("zh", "zl", "yh", "c"), [(source, target + 1) for source, target in sources]
    )

    w_other = lax.all_gather(partner, z, axis=0, tiled=True)

    place = jnp.stack([core, lax.axis_index("yh").astype(jnp.int32)])

    def partial(name, first, columns, *operands):
        return pl.pallas_call(
            functools.partial(partial_kernel, first),
            out_shape=jax.ShapeDtypeStruct((4, HALO + group_rows, columns), bf16),
            in_specs=[smem] + [vmem] * len(operands),
            out_specs=vmem,
            compiler_params=params,
            name=name,
        )(place, *operands)

    s_part = partial("partial_s", 512, HD, own_t, other_t, tail, w_own, w_other)
    tail, s_part = lax.optimization_barrier((tail, s_part))
    s_parts = lax.all_to_all(s_part, "x", 0, 0)
    qx_part = partial("partial_qx", 0, 512, own_t, other_t, tail, w_own, w_other)
    s_parts, qx_part = lax.optimization_barrier((s_parts, qx_part))
    qx_parts = lax.all_to_all(qx_part, "x", 0, 0)
    s_own = jnp.sum(s_parts.astype(jnp.float32), axis=0).astype(bf16)
    extra = jnp.stack([positions >> 8, positions & 255, offsets >> 8, offsets & 255], axis=1)
    extra = jnp.pad(extra, ((0, 0), (0, HD - 4))).astype(bf16)
    s_all = lax.all_gather(jnp.concatenate([s_own, extra], axis=0), ("yl", "c"), axis=0)
    qx_parts, s_all = lax.optimization_barrier((qx_parts, s_all))

    places = s_all[:, HALO + group_rows :, :4].reshape(group_rows, 4).astype(jnp.float32)
    half = HD // 2
    index = jnp.arange(half, dtype=jnp.float32)
    inverse = jnp.exp(-jnp.log(jnp.float32(rope_base)) * index / jnp.float32(half))
    angle = (places[:, 0] * 256.0 + places[:, 1])[:, None] * inverse[None, :]
    cosine, sine = jnp.cos(angle), jnp.sin(angle)
    cosine = jnp.concatenate([cosine, cosine], axis=1)
    sine = jnp.concatenate([-sine, sine], axis=1)
    starts = (places[:, 2] * 256.0 + places[:, 3]).astype(jnp.int32)
    row_ids = lax.axis_index(FSDP) * group_rows + jnp.arange(group_rows, dtype=jnp.int32)
    rel = jnp.broadcast_to((row_ids - starts)[:, None], (group_rows, HD))

    return pl.pallas_call(
        final_kernel,
        out_shape=(
            jax.ShapeDtypeStruct((group_rows, 256), bf16),
            jax.ShapeDtypeStruct((group_rows, 512), bf16),
            jax.ShapeDtypeStruct((group_rows, 256), bf16),
            jax.ShapeDtypeStruct((group_rows, 512), bf16),
        ),
        in_specs=[vmem] * 7,
        out_specs=(vmem,) * 4,
        scratch_shapes=[pltpu.VMEM((group_rows + HALO, HD), jnp.float32)],
        compiler_params=params,
        name="rotate_and_convolve",
    )(qx_parts, s_all, cosine, sine, rel, conv_x, conv_bc)


def solution(mesh):
    chips = Mesh(mesh.devices.reshape(SIZES), AXES)
    head = ("yl", "c")
    in_specs = (
        P(AXES, None), P(AXES), P(AXES),
        P(FSDP, head), P(FSDP, head), P(FSDP, head),
        P(None, head), P(),
    )
    out_specs = (P(FSDP, head), P(FSDP, None), P(FSDP, head), P(FSDP, None))
    return jax.shard_map(shards, mesh=chips, in_specs=in_specs, out_specs=out_specs, check_vma=False)
```
